128 devices in a mesh: slab: 16 (over x, z), sta: 8 (over y, core).
Axes of the slice: x: 4, y: 4, z: 4, core: 2. Of those that a mesh axis runs over, the one named last changes fastest.
Arguments:
- model_change: float32 [4, 192, 256, 256], P(None, 'slab', 'sta'), may hold values from -6 to 6
- sens_blocks: bfloat16 [16, 8, 640, 128, 128], P('slab', 'sta'), may hold values from -0.01953125 to 0.01953125
- block_rows: int32 [16, 8, 640], P('slab', 'sta'), may hold values from 0 to 127
- block_cols: int32 [16, 8, 640], P('slab', 'sta'), may hold values from 0 to 12287, as said below
- live_count: int32 [16, 8], P('slab', 'sta'), may hold values from 320 to 640, as said below
- owner_order: int32 [128], replicated, may hold values from 0 to 127, each once
Outputs:
- gravity_data: float32 [4, 16384], P(None, ('slab', 'sta'))
The draws below stay inside these ranges and needn't reach their ends.
Inputs may be any that keep to these rules, and one draw needn't show every extreme that they name: `block_cols`: among one device's 640 entries at most 80 name blocks p * 768 + b of one p, and on every device exactly 80 do for some p. `live_count`: some device has all 640 entries live.
All inputs are finite; a program needn't handle non-finite values.
Results may differ from the reference program's by a relative error of at most 0.0029.
Values may be sent and summed in bfloat16 or wider, within the bound.
A program may use at most 128 MiB of HBM per device.

```python
import math
import jax
import jax.numpy as jnp
from jax import lax

EPOCHS = 4
BLK = 128
NZ = 256
SX = 12
SY = 32
K = 640
CAP = 80
NX = 192
NY = 256
CB_DEV = 768
NSB = 128
N_SLAB = 16
N_STA = 8


def draw_block_cols(key, part):
    key = jax.random.fold_in(key, 11)
    device_total = N_SLAB * N_STA
    key_list = jax.random.split(key, device_total)

    def per_device(sub_key, device_index):
        key_full, key_order, key_mix, key_local = jax.random.split(sub_key, 4)
        random_peer = jax.random.randint(key_full, (), 0, N_SLAB)
        full_peer = jnp.where(device_index == 0, N_SLAB - 1, jnp.where(device_index == 1, 0, random_peer)).astype(jnp.int32)
        slot_ids = jnp.arange(N_SLAB * CAP, dtype=jnp.int32)
        slot_score = jax.random.permutation(key_order, N_SLAB * CAP).astype(jnp.int32)
        slot_score = jnp.where(slot_ids // CAP == full_peer, -1 - slot_ids, slot_score)
        chosen = jnp.argsort(slot_score, stable=True)[:K].astype(jnp.int32)
        chosen = jax.random.permutation(key_mix, chosen)
        peer_of = chosen // CAP
        local_block = jax.random.randint(key_local, (K,), 0, CB_DEV).astype(jnp.int32)
        first_full = jnp.argmax((peer_of == full_peer).astype(jnp.int32))
        forced = jnp.where(device_index == 0, CB_DEV - 1, jnp.where(device_index == 1, 0, local_block[first_full])).astype(jnp.int32)
        local_block = jnp.where(jnp.arange(K, dtype=jnp.int32) == first_full, forced, local_block)
        return peer_of * CB_DEV + local_block
    result = jax.vmap(per_device)(key_list, jnp.arange(device_total, dtype=jnp.int32))
    return result.reshape(N_SLAB, N_STA, K).astype(jnp.int32)


def draw_live_count(key, part):
    key = jax.random.fold_in(key, 23)
    key_count, key_spot = jax.random.split(key)
    device_total = N_SLAB * N_STA
    counts = jax.random.randint(key_count, (device_total,), K // 2, K + 1)
    full_device = jax.random.randint(key_spot, (), 0, device_total)
    counts = jnp.where(jnp.arange(device_total) == full_device, K, counts)
    return counts.reshape(N_SLAB, N_STA).astype(jnp.int32)


def with_ends(drawn, rng, smallest, largest):
    dims = drawn.shape
    index_at = [jax.random.randint(jax.random.fold_in(rng, axis), (), 0, dims[axis]) for axis in range(len(dims))]
    drawn = drawn.at[tuple(index_at)].set(smallest)
    longest = dims.index(max(dims))
    index_at[longest] = (index_at[longest] + 1) % dims[longest]
    return drawn.at[tuple(index_at)].set(largest)


def block_levels(own_key, extent, pieces, low, high):
    loudness = 1.0
    for axis_at, blocks in pieces:
        steps = jax.random.uniform(jax.random.fold_in(jax.random.fold_in(own_key, 6), axis_at), (blocks,), jnp.float32, low / len(pieces), high / len(pieces))
        loudness = loudness * jnp.repeat(jnp.exp(steps), extent[axis_at] // blocks).reshape((-1,) + (1,) * (len(extent) - 1 - axis_at))
    return loudness


def gaussian(key, dims, deviation, limit, shards=(), kind=jnp.bfloat16):
    level = block_levels(key, dims, shards, -0.22, 0.18) if shards else 1.0
    entries = jax.random.normal(key, dims, jnp.float32) * deviation * level
    return jnp.minimum(jnp.maximum(entries, -limit), limit).astype(kind)


def setup_inputs(seed: int = 0) -> dict:
    key_of = jax.random.split(jax.random.key(seed), 7)
    model_change = gaussian(key_of[0], (EPOCHS, NX, NY, NZ), 1.0, 6.0, ((1, 16), (2, 8)), jnp.float32)
    sens_blocks = gaussian(key_of[1], (N_SLAB, N_STA, K, BLK, BLK), (BLK * K) ** -0.5, 0.01953125, ((0, 16), (1, 8)))
    block_rows = with_ends(jax.random.randint(key_of[2], (N_SLAB, N_STA, K), 0, NSB), jax.random.fold_in(key_of[2], 1), 0, NSB - 1).astype(jnp.int32)
    block_cols = draw_block_cols(jax.random.fold_in(key_of[6], 71), 0)
    live_count = draw_live_count(jax.random.fold_in(key_of[6], 71), 0)
    owner_order = jax.random.permutation(key_of[5], NSB).astype(jnp.int32)
    return {"model_change": model_change, "sens_blocks": sens_blocks, "block_rows": block_rows, "block_cols": block_cols, "live_count": live_count, "owner_order": owner_order}


FILTER_TAPS = ((1.0 + math.sqrt(3.0)) / (4.0 * math.sqrt(2.0)), (3.0 + math.sqrt(3.0)) / (4.0 * math.sqrt(2.0)), (3.0 - math.sqrt(3.0)) / (4.0 * math.sqrt(2.0)), (1.0 - math.sqrt(3.0)) / (4.0 * math.sqrt(2.0)))

def wavelet_axis(values, along):
    length = values.shape[along]
    even_cells = lax.slice_in_dim(values, 0, length, 2, along)
    odd_cells = lax.slice_in_dim(values, 1, length, 2, along)
    next_even = jnp.roll(even_cells, -1, along)
    next_odd = jnp.roll(odd_cells, -1, along)
    low_band = FILTER_TAPS[0] * even_cells + FILTER_TAPS[1] * odd_cells + FILTER_TAPS[2] * next_even + FILTER_TAPS[3] * next_odd
    high_band = FILTER_TAPS[3] * even_cells - FILTER_TAPS[2] * odd_cells + FILTER_TAPS[1] * next_even - FILTER_TAPS[0] * next_odd
    return jnp.stack([low_band, high_band], along + 1).reshape(values.shape)

def reference(model_change, sens_blocks, block_rows, block_cols, live_count, owner_order):
    wave_field = model_change
    for along in (3, 2, 1):
        wave_field = wavelet_axis(wave_field, along)
    coef_all = wave_field.astype(jnp.bfloat16)
    block_count = SX * SY * NZ // BLK
    column_view = coef_all.reshape(EPOCHS, N_SLAB, SX, N_STA, SY, NZ).transpose(3, 0, 1, 2, 4, 5)
    column_view = column_view.reshape(N_STA, EPOCHS, N_SLAB * block_count, BLK)
    entry_index = jnp.arange(K, dtype=jnp.int32)

    def per_device(totals, flat_index):
        slab_index = flat_index // N_STA
        sta_index = flat_index % N_STA
        blocks = sens_blocks[slab_index, sta_index]
        picked = jnp.take(column_view[sta_index], block_cols[slab_index, sta_index], axis=1)
        block_terms = jnp.einsum('ekc,ksc->kes', picked.astype(jnp.float32), blocks.astype(jnp.float32), precision=lax.Precision.HIGHEST)
        keep_mask = entry_index < live_count[slab_index, sta_index]
        route_table = ((owner_order[:, None] == block_rows[slab_index, sta_index][None, :]) & keep_mask[None, :]).astype(jnp.float32)
        totals = totals + jnp.einsum('bk,kes->ebs', route_table, block_terms, precision=lax.Precision.HIGHEST)
        return (totals, None)
    totals, _ = lax.scan(per_device, jnp.zeros((EPOCHS, NSB, BLK), jnp.float32), jnp.arange(N_SLAB * N_STA, dtype=jnp.int32))
    return totals.reshape(EPOCHS, NSB * BLK)
```

```python
import functools
import math

import jax
import jax.numpy as jnp
import ml_dtypes
import numpy as np
from jax import lax
from jax.experimental import pallas as pl
from jax.experimental.pallas import tpu as pltpu
from jax.sharding import PartitionSpec as P

MESH = pl.DeviceIdType.MESH
F32, BF16, I32 = jnp.float32, jnp.bfloat16, jnp.int32
NT = (((1,), (1,)), ((), ()))
R3 = math.sqrt(3.0)
H0, H1, H2, H3 = (
    (1.0 + R3) / (4.0 * math.sqrt(2.0)),
    (3.0 + R3) / (4.0 * math.sqrt(2.0)),
    (3.0 - R3) / (4.0 * math.sqrt(2.0)),
    (1.0 - R3) / (4.0 * math.sqrt(2.0)),
)
C1, C2 = H3 / H0, H1 / H2

EP, SX, SY, NZ, BLK = 4, 12, 32, 256, 128
K, CAP, CB = 640, 80, 768
NSLAB, NSTA = 16, 8
MSG = CAP * EP
KT = K // BLK


def torus(step):
    dx, dz = divmod(step, 4)
    return min(dx, 4 - dx) + min(dz, 4 - dz)


STEPS = [(0, 0)] + [divmod(s, 4) for s in sorted(range(1, 16), key=lambda s: -torus(s))]


def z_matrix():
    w = np.zeros((NZ, NZ), np.float64)
    for k in range(NZ // 2):
        src = [(2 * k + d) % NZ for d in range(4)]
        for at, lo, hi in zip(src, (H0, H1, H2, H3), (H3, -H2, H1, -H0)):
            w[at, 2 * k] = lo
            w[at, 2 * k + 1] = hi
    top = w.astype(ml_dtypes.bfloat16)
    rest = (w - top.astype(np.float64)).astype(ml_dtypes.bfloat16)
    return np.concatenate([top, top, rest], 0)


def behind_of(i, n):
    dx, dz = STEPS[n]
    return lax.rem(i // 4 + 4 - dx, 4) * 4 + lax.rem(lax.rem(i, 4) + 4 - dz, 4)


def list_kernel(cols, rows, live, owner, req, lists, R):
    i = lax.axis_index("slab")
    behind = functools.partial(behind_of, i)
    sub16 = lax.broadcasted_iota(I32, (16, BLK), 0)
    sub128 = lax.broadcasted_iota(I32, (BLK, BLK), 0)
    lane128 = lax.broadcasted_iota(I32, (BLK, BLK), 1)
    sub8 = lax.broadcasted_iota(I32, (8, BLK), 0)
    lane8 = lax.broadcasted_iota(I32, (8, BLK), 1)
    one = lambda m: jnp.where(m, 1.0, 0.0).astype(BF16)
    peer = jnp.zeros((16, BLK), I32)
    for n in range(NSLAB):
        peer = jnp.where(sub16 == n, behind(n), peer)
    first = peer * CB
    upper = one(sub128 < lane128)
    ties, ranks, rels = [], [], []
    carry = jnp.zeros((16, 1), F32)
    for t in range(KT):
        rel = cols[:, t * BLK : (t + 1) * BLK] - first
        tie = (rel >= 0) & (rel < CB)
        tie_f = jnp.where(tie, 1.0, 0.0)
        ranks.append(jnp.dot(tie_f.astype(BF16), upper, preferred_element_type=F32) + carry)
        carry = carry + jnp.sum(tie_f, axis=1, keepdims=True)
        ties.append(tie_f)
        rels.append(jnp.where(tie, rel, 0))
    count = jnp.broadcast_to(carry, (16, BLK))
    scan = count
    for s in (1, 2, 4, 8):
        scan = scan + jnp.where(sub16 >= s, pltpu.roll(scan, s, 0), 0.0)
    base = scan - count

    place = one(sub128 == owner[...])
    inverse = lax.dot_general(
        lane8.astype(F32).astype(BF16), place, NT, preferred_element_type=F32
    ).astype(BF16)
    live_now = live[0, 0]
    ask = jnp.zeros((32, BLK), F32)
    vals, spots = [], []
    for t in range(KT):
        rank_k = jnp.sum(ties[t] * ranks[t], axis=0, keepdims=True).astype(I32)
        slot_k = jnp.sum(ties[t] * (ranks[t] + sub16.astype(F32) * CAP), axis=0, keepdims=True).astype(I32)
        spots.append(jnp.sum(ties[t] * (ranks[t] + base), axis=0, keepdims=True).astype(I32))
        rel = rels[t]
        cell = (rel & -64) + ((rel & 1) << 5) + ((rel >> 1) & 31)
        pair = jnp.concatenate([(cell >> 3).astype(F32), (cell & 7).astype(F32)], 0).astype(BF16)
        ask = ask + lax.dot_general(pair, one(sub128 == rank_k), NT, preferred_element_type=F32)
        dest = jnp.dot(
            inverse, one(sub128 == rows[:, t * BLK : (t + 1) * BLK]), preferred_element_type=F32
        )
        here = lane8 + t * BLK
        dest = jnp.where(here < live_now, dest, 128.0)
        slot8 = jnp.broadcast_to(slot_k, (8, BLK))
        val = jnp.where(sub8 == 0, here >> 3, here & 7)
        val = jnp.where(sub8 == 2, slot8 >> 3, val)
        val = jnp.where(sub8 == 3, slot8 & 7, val).astype(F32)
        vals.append(jnp.where(sub8 == 4, dest, val).astype(BF16))
    ask = (ask[:16] * 8.0 + ask[16:]).astype(I32)
    for n in range(NSLAB):
        req[n] = ask[n : n + 1]

    for u in range(KT):
        got = jnp.zeros((8, BLK), F32)
        for t in range(KT):
            got = got + lax.dot_general(
                vals[t], one(sub128 + u * BLK == spots[t]), NT, preferred_element_type=F32
            )
        dest = got[4:5].astype(I32)
        R[:, u * BLK : (u + 1) * BLK] = one(sub128 == dest)
        lists[0:1, u * BLK : (u + 1) * BLK] = (got[0:1] * 8.0 + got[1:2]).astype(I32)
        lists[1:2, u * BLK : (u + 1) * BLK] = (got[2:3] * 8.0 + got[3:4]).astype(I32)


def kernel(
    model, sens, req, lists, route_in, wz, out,
    X, sv, wv, Sx, Sy, Sc, Rx, Ry, Rc, D, C, st, send, recv, work, gat, T, R,
    reqin, reqs, lists_s, red, redin, acc, accin,
    lsem, hss, hrs, qss, qrs, ass_, ars, rss, rrs, tss, trs,
):
    i, j = lax.axis_index("slab"), lax.axis_index("sta")
    xx, zz = i // 4, lax.rem(i, 4)

    loads = [
        pltpu.make_async_copy(src, dst, lsem.at[n])
        for n, (src, dst) in enumerate(
            ((model, X), (req.at[0], reqin.at[0]), (wz, wv), (lists, lists_s), (route_in, R), (sens, sv))
        )
    ]
    for cp in loads:
        cp.start()

    def ahead(n):
        dx, dz = STEPS[n]
        return lax.rem(xx + dx, 4) * 4 + lax.rem(zz + dz, 4)

    behind = functools.partial(behind_of, i)

    up_i, down_i = lax.rem(i + 1, NSLAB), lax.rem(i + NSLAB - 1, NSLAB)
    up_j, down_j = lax.rem(j + 1, NSTA), lax.rem(j + NSTA - 1, NSTA)

    bar = pltpu.get_barrier_semaphore()
    for n in range(1, NSLAB):
        pl.semaphore_signal(bar, inc=1, device_id=(ahead(n), j), device_id_type=MESH)
    for t in range(1, NSTA):
        pl.semaphore_signal(bar, inc=1, device_id=(i, lax.rem(j + t, NSTA)), device_id_type=MESH)
    pl.semaphore_signal(bar, inc=1, device_id=(up_i, up_j), device_id_type=MESH)

    loads[0].wait()
    for e in range(EP):
        Sx[e] = H2 * X[e, 0] + H3 * X[e, 1]
    for e in range(EP):
        for x in range(SX):
            Sy[4 * x + e : 4 * x + e + 1, :] = H2 * X[e, x, 0:1, :] + H3 * X[e, x, 1:2, :]
    Sc[0:4, :] = H2 * Sy[0:4, :] + H3 * Sy[4:8, :]
    Sc[4:8, :] = jnp.zeros((4, NZ), F32)

    pl.semaphore_wait(bar, NSLAB - 1 + NSTA - 1 + 1)
    halos = [
        pltpu.make_async_remote_copy(src, dst, hss.at[n], hrs.at[n], device_id=dev, device_id_type=MESH)
        for n, (src, dst, dev) in enumerate(
            ((Sy, Ry, (i, down_j)), (Sc, Rc, (down_i, down_j)), (Sx, Rx, (down_i, j)))
        )
    ]
    for cp in halos:
        cp.start()
    asks = [
        pltpu.make_async_remote_copy(
            req.at[n], reqin.at[n], qss.at[n], qrs.at[n], device_id=(behind(n), j), device_id_type=MESH
        )
        for n in range(1, NSLAB)
    ]
    for cp in asks:
        cp.start()

    def spread(x, e, q, val):
        for z in range(2):
            D[z, x, pl.ds(32 * q + e, 8, stride=4), :] = val[:, z * BLK : (z + 1) * BLK]

    def x_pair(k, _):
        for e in range(EP):
            for q in range(SY // 8):
                at = slice(8 * q, 8 * q + 8)
                s = H0 * X[e, 2 * k, at, :] + H1 * X[e, 2 * k + 1, at, :]
                t = H2 * X[e, 2 * k + 2, at, :] + H3 * X[e, 2 * k + 3, at, :]
                spread(2 * k, e, q, s + t)
                spread(2 * k + 1, e, q, C1 * s + C2 * t)
        return 0

    lax.fori_loop(0, SX // 2 - 1, x_pair, 0)

    halos[0].wait_recv()
    halos[1].wait_recv()
    for k in range(SX // 2):
        s = H0 * Ry[8 * k : 8 * k + 4, :] + H1 * Ry[8 * k + 4 : 8 * k + 8, :]
        if k < SX // 2 - 1:
            t = H2 * Ry[8 * k + 8 : 8 * k + 12, :] + H3 * Ry[8 * k + 12 : 8 * k + 16, :]
        else:
            t = Rc[0:4, :]
        lo, hi = s + t, C1 * s + C2 * t
        for z in range(2):
            at = slice(z * BLK, (z + 1) * BLK)
            D[z, 2 * k, SY * 4 : SY * 4 + 4, :] = lo[:, at]
            D[z, 2 * k + 1, SY * 4 : SY * 4 + 4, :] = hi[:, at]

    low = lax.broadcasted_iota(I32, (8, BLK), 0) < 4
    ca, cb = jnp.where(low, H0, -H2), jnp.where(low, H1, H3)
    cc, cd = jnp.where(low, H2, -H0), jnp.where(low, H3, H1)
    ce = jnp.where(low, 1.0, C2)
    loads[2].wait()

    def yz(x, _):
        parts = []
        for z in range(2):
            v = D[z, x, 0 : SY * 4, :].reshape(SY // 2, 8, BLK)
            u = pltpu.roll(v, 4, 1)
            s = ca * v + cb * u
            t = cc * v[1:] + cd * u[1:]
            rim = D[z, x, SY * 4 : SY * 4 + 4, :]
            last = ce * jnp.concatenate([rim, rim], 0)
            parts.append((s + jnp.concatenate([t, last[None]], 0)).reshape(SY * 4, BLK))
        full = jnp.concatenate(parts, 1)
        high = full.astype(BF16)
        rest = (full - high.astype(F32)).astype(BF16)
        res = jnp.dot(jnp.concatenate([high, rest, high], 1), wv[...], preferred_element_type=F32)
        at = pl.multiple_of(x * 2 * SY * 4, 2 * SY * 4)
        C[pl.ds(at, SY * 4), :] = res[:, :BLK]
        C[pl.ds(at + SY * 4, SY * 4), :] = res[:, BLK:]
        return 0

    lax.fori_loop(0, SX - 2, yz, 0)
    halos[2].wait_recv()
    for e in range(EP):
        for q in range(SY // 8):
            at = slice(8 * q, 8 * q + 8)
            s = H0 * X[e, SX - 2, at, :] + H1 * X[e, SX - 1, at, :]
            t = Rx[e, at, :]
            spread(SX - 2, e, q, s + t)
            spread(SX - 1, e, q, C1 * s + C2 * t)
    lax.fori_loop(SX - 2, SX, yz, 0)

    loads[1].wait()
    for cp in asks:
        cp.wait_recv()
    to_r = pltpu.make_async_copy(reqin, reqs, lsem.at[8])
    to_r.start()
    to_r.wait()
    loads[3].wait()

    def pack(n):
        def some(g, _):
            for a in range(8):
                c = reqs[n, 0, g * 8 + a]
                st[g, 4 * a : 4 * a + 4, :] = C[pl.ds(c * 4, 4), :]
            return 0

        lax.fori_loop(0, CAP // 8, some, 0)

    msgs = []
    for n in list(range(1, NSLAB)) + [0]:
        pack(n)
        if n == 0:
            work[0:MSG, :] = st[...].reshape(MSG, BLK).astype(BF16).astype(F32)
            break
        send[n] = st[...].reshape(MSG, BLK).astype(BF16)
        cp = pltpu.make_async_remote_copy(
            send.at[n], recv.at[n], ass_.at[n], ars.at[n], device_id=(ahead(n), j), device_id_type=MESH
        )
        cp.start()
        msgs.append(cp)

    loads[5].wait()
    loads[4].wait()
    first_half = lax.broadcasted_iota(I32, (8, BLK), 0) < 4
    HALF = CAP // 2

    def products(g, _):
        for a in range(HALF):
            c = lists_s[1, g * HALF + a]
            gat[4 * a : 4 * a + 4, :] = work[pl.ds(c * 4, 4), :]
        for a in range(0, HALF, 2):
            lhs = gat[4 * a : 4 * a + 8, :].astype(BF16)
            rhs = jnp.concatenate([sv[lists_s[0, g * HALF + a]], sv[lists_s[0, g * HALF + a + 1]]], 0)
            res = lax.dot_general(lhs, rhs, NT, preferred_element_type=F32)
            at = pl.multiple_of(g * HALF * 4, HALF * 4) + 4 * a
            T[pl.ds(at, 8), :] = jnp.where(first_half, res[:, :BLK], res[:, BLK:])
        return 0

    def route(lo, hi):
        sums = []
        for e in range(EP):
            term = T[pl.ds(lo * 4 + e, hi - lo, stride=4), :]
            high = term.astype(BF16)
            rest = (term - high.astype(F32)).astype(BF16)
            r = R[:, lo:hi]
            sums.append(
                jnp.dot(r, high, preferred_element_type=F32) + jnp.dot(r, rest, preferred_element_type=F32)
            )
        return sums

    for n in range(1, NSLAB):
        msgs[n - 1].wait_recv()
        work[n * MSG : (n + 1) * MSG, :] = recv[n].astype(F32)
        if n >= NSLAB // 2:
            c = n - NSLAB // 2
            lax.fori_loop(2 * c, 2 * c + 2, products, 0)
        if n == NSLAB - 2:
            for e, part in enumerate(route(0, 512)):
                red[pl.ds(e, BLK, stride=4), :] = part
    for e, part in enumerate(route(512, K)):
        red[pl.ds(e, BLK, stride=4), :] = red[pl.ds(e, BLK, stride=4), :] + part

    sums = []
    for n in range(1, NSLAB):
        p = ahead(n)
        cp = pltpu.make_async_remote_copy(
            red.at[pl.ds(pl.multiple_of(p * 32, 32), 32), :], redin.at[n],
            rss.at[n], rrs.at[n], device_id=(p, j), device_id_type=MESH,
        )
        cp.start()
        sums.append(cp)
    total = red[pl.ds(pl.multiple_of(i * 32, 32), 32), :]
    for n in range(1, NSLAB):
        sums[n - 1].wait_recv()
        total = total + redin[n]
    for q in range(NSTA):
        acc[q] = total[4 * q : 4 * q + 4]
    lasts = []
    for t in range(1, NSTA):
        q = lax.rem(j + t, NSTA)
        cp = pltpu.make_async_remote_copy(
            acc.at[q], accin.at[t], tss.at[t], trs.at[t], device_id=(i, q), device_id_type=MESH
        )
        cp.start()
        lasts.append(cp)
    final = acc[j]
    for t in range(1, NSTA):
        lasts[t - 1].wait_recv()
        final = final + accin[t]
    out[...] = final
    for cp in halos + asks + msgs + sums + lasts:
        cp.wait_send()


def on_device(model_change, sens_blocks, block_rows, block_cols, live_count, owner_order):
    anyspace = pl.BlockSpec(memory_space=pl.ANY)
    dma = pltpu.SemaphoreType.DMA
    vm = pltpu.VMEM
    req, lists, routes = pl.pallas_call(
        list_kernel,
        out_shape=(
            jax.ShapeDtypeStruct((NSLAB, 1, BLK), I32),
            jax.ShapeDtypeStruct((2, K), I32),
            jax.ShapeDtypeStruct((BLK, K), BF16),
        ),
        in_specs=[
            pl.BlockSpec(memory_space=pltpu.SMEM if n == 2 else pltpu.VMEM) for n in range(4)
        ],
        out_specs=[pl.BlockSpec(memory_space=pltpu.VMEM)] * 3,
        name="lists",
    )(
        block_cols.reshape(1, K),
        block_rows.reshape(1, K),
        live_count.reshape(1, 1),
        owner_order.reshape(1, BLK),
    )
    return pl.pallas_call(
        kernel,
        out_shape=jax.ShapeDtypeStruct((EP, BLK), F32),
        in_specs=[anyspace] * 6,
        out_specs=pl.BlockSpec(memory_space=pltpu.VMEM),
        scratch_shapes=[
            vm((EP, SX, SY, NZ), F32), vm((K, BLK, BLK), BF16), vm((3 * NZ, NZ), BF16),
            vm((EP, SY, NZ), F32), vm((SX * 4, NZ), F32), vm((8, NZ), F32),
            vm((EP, SY, NZ), F32), vm((SX * 4, NZ), F32), vm((8, NZ), F32),
            vm((2, SX, SY * 4 + 8, BLK), F32), vm((CB * 4, BLK), F32),
            vm((CAP // 8, 32, BLK), F32), vm((NSLAB, MSG, BLK), BF16), vm((NSLAB, MSG, BLK), BF16),
            vm((NSLAB * MSG, BLK), F32), vm((MSG // 2, BLK), F32), vm((K * 4, BLK), F32), vm((BLK, K), BF16),
            vm((NSLAB, 1, BLK), I32), pltpu.SMEM((NSLAB, 1, BLK), I32),
            pltpu.SMEM((2, K), I32),
            vm((BLK * 4, BLK), F32), vm((NSLAB, 32, BLK), F32),
            vm((NSTA, 4, BLK), F32), vm((NSTA, 4, BLK), F32),
            dma((9,)), dma((3,)), dma((3,)), dma((NSLAB,)), dma((NSLAB,)), dma((NSLAB,)), dma((NSLAB,)),
            dma((NSLAB,)), dma((NSLAB,)), dma((NSTA,)), dma((NSTA,)),
        ],
        compiler_params=pltpu.CompilerParams(
            collective_id=0, has_side_effects=True, vmem_limit_bytes=52 * 2**20
        ),
        name="gravity_step",
    )(
        model_change,
        sens_blocks.reshape(K, BLK, BLK),
        req,
        lists,
        routes,
        jnp.asarray(z_matrix()),
    )


def solution(mesh):
    placed = (
        P(None, "slab", "sta", None),
        P("slab", "sta", None, None, None),
        P("slab", "sta", None),
        P("slab", "sta", None),
        P("slab", "sta"),
        P(),
    )
    return jax.shard_map(
        on_device, mesh=mesh, in_specs=placed, out_specs=P(None, ("slab", "sta")), check_vma=False
    )
```

```python
import functools
import math

import jax
import jax.numpy as jnp
import ml_dtypes
import numpy as np
from jax import lax
from jax.experimental import pallas as pl
from jax.experimental.pallas import tpu as pltpu
from jax.sharding import PartitionSpec as P

MESH = pl.DeviceIdType.MESH
F32, BF16, I32 = jnp.float32, jnp.bfloat16, jnp.int32
NT = (((1,), (1,)), ((), ()))
R3 = math.sqrt(3.0)
H0, H1, H2, H3 = (
    (1.0 + R3) / (4.0 * math.sqrt(2.0)),
    (3.0 + R3) / (4.0 * math.sqrt(2.0)),
    (3.0 - R3) / (4.0 * math.sqrt(2.0)),
    (1.0 - R3) / (4.0 * math.sqrt(2.0)),
)
C1, C2 = H3 / H0, H1 / H2

EP, SX, SY, NZ, BLK = 4, 12, 32, 256, 128
K, CAP, CB = 640, 80, 768
NSLAB, NSTA = 16, 8
MSG = CAP * EP
KT = K // BLK


def torus(step):
    dx, dz = divmod(step, 4)
    return min(dx, 4 - dx) + min(dz, 4 - dz)


STEPS = [(0, 0)] + [divmod(s, 4) for s in sorted(range(1, 16), key=lambda s: -torus(s))]


def z_matrix():
    w = np.zeros((NZ, NZ), np.float64)
    for k in range(NZ // 2):
        src = [(2 * k + d) % NZ for d in range(4)]
        for at, lo, hi in zip(src, (H0, H1, H2, H3), (H3, -H2, H1, -H0)):
            w[at, 2 * k] = lo
            w[at, 2 * k + 1] = hi
    top = w.astype(ml_dtypes.bfloat16)
    rest = (w - top.astype(np.float64)).astype(ml_dtypes.bfloat16)
    return np.concatenate([top, top, rest], 0)


def kernel(
    model, sens, cols, rows, live, owner, wz, out,
    X, sv, wv, cv, rv, ov, lv, Sx, Sy, Sc, Rx, Ry, Rc, D, C, st, send, recv, work, gat, T, R,
    reqv, reqin, reqs, lists, lists_s, red, redin, acc, accin,
    lsem, hss, hrs, qss, qrs, ass_, ars, rss, rrs, tss, trs,
):
    i, j = lax.axis_index("slab"), lax.axis_index("sta")
    xx, zz = i // 4, lax.rem(i, 4)

    loads = [
        pltpu.make_async_copy(src, dst, lsem.at[n])
        for n, (src, dst) in enumerate(
            ((cols, cv), (rows, rv), (owner, ov), (live, lv), (model, X), (wz, wv), (sens, sv))
        )
    ]
    for cp in loads:
        cp.start()

    def ahead(n):
        dx, dz = STEPS[n]
        return lax.rem(xx + dx, 4) * 4 + lax.rem(zz + dz, 4)

    def behind(n):
        dx, dz = STEPS[n]
        return lax.rem(xx + 4 - dx, 4) * 4 + lax.rem(zz + 4 - dz, 4)

    up_i, down_i = lax.rem(i + 1, NSLAB), lax.rem(i + NSLAB - 1, NSLAB)
    up_j, down_j = lax.rem(j + 1, NSTA), lax.rem(j + NSTA - 1, NSTA)

    bar = pltpu.get_barrier_semaphore()
    for n in range(1, NSLAB):
        pl.semaphore_signal(bar, inc=1, device_id=(ahead(n), j), device_id_type=MESH)
    for t in range(1, NSTA):
        pl.semaphore_signal(bar, inc=1, device_id=(i, lax.rem(j + t, NSTA)), device_id_type=MESH)
    pl.semaphore_signal(bar, inc=1, device_id=(up_i, up_j), device_id_type=MESH)

    for cp in loads[:4]:
        cp.wait()
    sub16 = lax.broadcasted_iota(I32, (16, BLK), 0)
    sub128 = lax.broadcasted_iota(I32, (BLK, BLK), 0)
    lane128 = lax.broadcasted_iota(I32, (BLK, BLK), 1)
    sub8 = lax.broadcasted_iota(I32, (8, BLK), 0)
    lane8 = lax.broadcasted_iota(I32, (8, BLK), 1)
    one = lambda m: jnp.where(m, 1.0, 0.0).astype(BF16)
    peer = jnp.zeros((16, BLK), I32)
    for n in range(NSLAB):
        peer = jnp.where(sub16 == n, behind(n), peer)
    first = peer * CB
    upper = one(sub128 < lane128)
    ties, ranks, rels = [], [], []
    carry = jnp.zeros((16, 1), F32)
    for t in range(KT):
        rel = cv[:, t * BLK : (t + 1) * BLK] - first
        tie = (rel >= 0) & (rel < CB)
        tie_f = jnp.where(tie, 1.0, 0.0)
        ranks.append(jnp.dot(tie_f.astype(BF16), upper, preferred_element_type=F32) + carry)
        carry = carry + jnp.sum(tie_f, axis=1, keepdims=True)
        ties.append(tie_f)
        rels.append(jnp.where(tie, rel, 0))
    count = jnp.broadcast_to(carry, (16, BLK))
    scan = count
    for s in (1, 2, 4, 8):
        scan = scan + jnp.where(sub16 >= s, pltpu.roll(scan, s, 0), 0.0)
    base = scan - count

    place = one(sub128 == ov[...])
    inverse = lax.dot_general(
        lane8.astype(F32).astype(BF16), place, NT, preferred_element_type=F32
    ).astype(BF16)
    live_now = lv[0, 0]
    ask = jnp.zeros((32, BLK), F32)
    vals, spots = [], []
    for t in range(KT):
        rank_k = jnp.sum(ties[t] * ranks[t], axis=0, keepdims=True).astype(I32)
        slot_k = jnp.sum(ties[t] * (jnp.minimum(ranks[t], CAP - 1.0) + sub16.astype(F32) * CAP), axis=0, keepdims=True).astype(I32)
        spots.append(jnp.sum(ties[t] * (ranks[t] + base), axis=0, keepdims=True).astype(I32))
        rel = rels[t]
        cell = (rel & -64) + ((rel & 1) << 5) + ((rel >> 1) & 31)
        pair = jnp.concatenate([(cell >> 3).astype(F32), (cell & 7).astype(F32)], 0).astype(BF16)
        ask = ask + lax.dot_general(pair, one(sub128 == rank_k), NT, preferred_element_type=F32)
        dest = jnp.dot(
            inverse, one(sub128 == rv[:, t * BLK : (t + 1) * BLK]), preferred_element_type=F32
        )
        here = lane8 + t * BLK
        dest = jnp.where(here < live_now, dest, 128.0)
        slot8 = jnp.broadcast_to(slot_k, (8, BLK))
        val = jnp.where(sub8 == 0, here >> 3, here & 7)
        val = jnp.where(sub8 == 2, slot8 >> 3, val)
        val = jnp.where(sub8 == 3, slot8 & 7, val).astype(F32)
        vals.append(jnp.where(sub8 == 4, dest, val).astype(BF16))
    ask = jnp.clip((ask[:16] * 8.0 + ask[16:]).astype(I32), 0, CB - 1)
    for n in range(NSLAB):
        if n == 0:
            reqin[n] = ask[n : n + 1]
        else:
            reqv[n] = ask[n : n + 1]

    loads[4].wait()
    for e in range(EP):
        Sx[e] = H2 * X[e, 0] + H3 * X[e, 1]
    for e in range(EP):
        for x in range(SX):
            Sy[4 * x + e : 4 * x + e + 1, :] = H2 * X[e, x, 0:1, :] + H3 * X[e, x, 1:2, :]
    Sc[0:4, :] = H2 * Sy[0:4, :] + H3 * Sy[4:8, :]
    Sc[4:8, :] = jnp.zeros((4, NZ), F32)

    pl.semaphore_wait(bar, NSLAB - 1 + NSTA - 1 + 1)
    halos = [
        pltpu.make_async_remote_copy(src, dst, hss.at[n], hrs.at[n], device_id=dev, device_id_type=MESH)
        for n, (src, dst, dev) in enumerate(
            ((Sy, Ry, (i, down_j)), (Sc, Rc, (down_i, down_j)), (Sx, Rx, (down_i, j)))
        )
    ]
    for cp in halos:
        cp.start()
    asks = [
        pltpu.make_async_remote_copy(
            reqv.at[n], reqin.at[n], qss.at[n], qrs.at[n], device_id=(behind(n), j), device_id_type=MESH
        )
        for n in range(1, NSLAB)
    ]
    for cp in asks:
        cp.start()

    def spread(x, e, q, val):
        for z in range(2):
            D[z, x, pl.ds(32 * q + e, 8, stride=4), :] = val[:, z * BLK : (z + 1) * BLK]

    def x_pair(k, _):
        for e in range(EP):
            for q in range(SY // 8):
                at = slice(8 * q, 8 * q + 8)
                s = H0 * X[e, 2 * k, at, :] + H1 * X[e, 2 * k + 1, at, :]
                t = H2 * X[e, 2 * k + 2, at, :] + H3 * X[e, 2 * k + 3, at, :]
                spread(2 * k, e, q, s + t)
                spread(2 * k + 1, e, q, C1 * s + C2 * t)
        return 0

    lax.fori_loop(0, SX // 2 - 1, x_pair, 0)

    order = []
    for u in range(KT):
        got = jnp.zeros((8, BLK), F32)
        for t in range(KT):
            got = got + lax.dot_general(
                vals[t], one(sub128 + u * BLK == spots[t]), NT, preferred_element_type=F32
            )
        dest = got[4:5].astype(I32)
        R[:, u * BLK : (u + 1) * BLK] = one(sub128 == dest)
        lists[0:1, u * BLK : (u + 1) * BLK] = jnp.clip(
            (got[0:1] * 8.0 + got[1:2]).astype(I32), 0, K - 1
        )
        lists[1:2, u * BLK : (u + 1) * BLK] = jnp.clip(
            (got[2:3] * 8.0 + got[3:4]).astype(I32), 0, NSLAB * CAP - 1
        )
    to_s = pltpu.make_async_copy(lists, lists_s, lsem.at[7])
    to_s.start()

    halos[0].wait_recv()
    halos[1].wait_recv()
    for k in range(SX // 2):
        s = H0 * Ry[8 * k : 8 * k + 4, :] + H1 * Ry[8 * k + 4 : 8 * k + 8, :]
        if k < SX // 2 - 1:
            t = H2 * Ry[8 * k + 8 : 8 * k + 12, :] + H3 * Ry[8 * k + 12 : 8 * k + 16, :]
        else:
            t = Rc[0:4, :]
        lo, hi = s + t, C1 * s + C2 * t
        for z in range(2):
            at = slice(z * BLK, (z + 1) * BLK)
            D[z, 2 * k, SY * 4 : SY * 4 + 4, :] = lo[:, at]
            D[z, 2 * k + 1, SY * 4 : SY * 4 + 4, :] = hi[:, at]

    low = lax.broadcasted_iota(I32, (8, BLK), 0) < 4
    ca, cb = jnp.where(low, H0, -H2), jnp.where(low, H1, H3)
    cc, cd = jnp.where(low, H2, -H0), jnp.where(low, H3, H1)
    ce = jnp.where(low, 1.0, C2)
    loads[5].wait()

    def yz(x, _):
        parts = []
        for z in range(2):
            v = D[z, x, 0 : SY * 4, :].reshape(SY // 2, 8, BLK)
            u = pltpu.roll(v, 4, 1)
            s = ca * v + cb * u
            t = cc * v[1:] + cd * u[1:]
            rim = D[z, x, SY * 4 : SY * 4 + 4, :]
            last = ce * jnp.concatenate([rim, rim], 0)
            parts.append((s + jnp.concatenate([t, last[None]], 0)).reshape(SY * 4, BLK))
        full = jnp.concatenate(parts, 1)
        high = full.astype(BF16)
        rest = (full - high.astype(F32)).astype(BF16)
        res = jnp.dot(jnp.concatenate([high, rest, high], 1), wv[...], preferred_element_type=F32)
        at = pl.multiple_of(x * 2 * SY * 4, 2 * SY * 4)
        C[pl.ds(at, SY * 4), :] = res[:, :BLK]
        C[pl.ds(at + SY * 4, SY * 4), :] = res[:, BLK:]
        return 0

    lax.fori_loop(0, SX - 2, yz, 0)
    halos[2].wait_recv()
    for e in range(EP):
        for q in range(SY // 8):
            at = slice(8 * q, 8 * q + 8)
            s = H0 * X[e, SX - 2, at, :] + H1 * X[e, SX - 1, at, :]
            t = Rx[e, at, :]
            spread(SX - 2, e, q, s + t)
            spread(SX - 1, e, q, C1 * s + C2 * t)
    lax.fori_loop(SX - 2, SX, yz, 0)

    for cp in asks:
        cp.wait_recv()
    to_r = pltpu.make_async_copy(reqin, reqs, lsem.at[8])
    to_r.start()
    to_r.wait()
    to_s.wait()

    def pack(n):
        def some(g, _):
            for a in range(8):
                c = reqs[n, 0, g * 8 + a]
                st[g, 4 * a : 4 * a + 4, :] = C[pl.ds(c * 4, 4), :]
            return 0

        lax.fori_loop(0, CAP // 8, some, 0)

    msgs = []
    for n in list(range(1, NSLAB)) + [0]:
        pack(n)
        if n == 0:
            work[0:MSG, :] = st[...].reshape(MSG, BLK).astype(BF16).astype(F32)
            break
        send[n] = st[...].reshape(MSG, BLK).astype(BF16)
        cp = pltpu.make_async_remote_copy(
            send.at[n], recv.at[n], ass_.at[n], ars.at[n], device_id=(ahead(n), j), device_id_type=MESH
        )
        cp.start()
        msgs.append(cp)

    loads[6].wait()
    first_half = lax.broadcasted_iota(I32, (8, BLK), 0) < 4
    HALF = CAP // 2

    def products(g, _):
        for a in range(HALF):
            c = lists_s[1, g * HALF + a]
            gat[4 * a : 4 * a + 4, :] = work[pl.ds(c * 4, 4), :]
        for a in range(0, HALF, 2):
            lhs = gat[4 * a : 4 * a + 8, :].astype(BF16)
            rhs = jnp.concatenate([sv[lists_s[0, g * HALF + a]], sv[lists_s[0, g * HALF + a + 1]]], 0)
            res = lax.dot_general(lhs, rhs, NT, preferred_element_type=F32)
            at = pl.multiple_of(g * HALF * 4, HALF * 4) + 4 * a
            T[pl.ds(at, 8), :] = jnp.where(first_half, res[:, :BLK], res[:, BLK:])
        return 0

    def route(lo, hi):
        sums = []
        for e in range(EP):
            term = T[pl.ds(lo * 4 + e, hi - lo, stride=4), :]
            high = term.astype(BF16)
            rest = (term - high.astype(F32)).astype(BF16)
            r = R[:, lo:hi]
            sums.append(
                jnp.dot(r, high, preferred_element_type=F32) + jnp.dot(r, rest, preferred_element_type=F32)
            )
        return sums

    for n in range(1, NSLAB):
        msgs[n - 1].wait_recv()
        work[n * MSG : (n + 1) * MSG, :] = recv[n].astype(F32)
        if n >= NSLAB // 2:
            c = n - NSLAB // 2
            lax.fori_loop(2 * c, 2 * c + 2, products, 0)
        if n == NSLAB - 2:
            for e, part in enumerate(route(0, 512)):
                red[pl.ds(e, BLK, stride=4), :] = part
    for e, part in enumerate(route(512, K)):
        red[pl.ds(e, BLK, stride=4), :] = red[pl.ds(e, BLK, stride=4), :] + part

    sums = []
    for n in range(1, NSLAB):
        p = ahead(n)
        cp = pltpu.make_async_remote_copy(
            red.at[pl.ds(pl.multiple_of(p * 32, 32), 32), :], redin.at[n],
            rss.at[n], rrs.at[n], device_id=(p, j), device_id_type=MESH,
        )
        cp.start()
        sums.append(cp)
    total = red[pl.ds(pl.multiple_of(i * 32, 32), 32), :]
    for n in range(1, NSLAB):
        sums[n - 1].wait_recv()
        total = total + redin[n]
    for q in range(NSTA):
        acc[q] = total[4 * q : 4 * q + 4]
    lasts = []
    for t in range(1, NSTA):
        q = lax.rem(j + t, NSTA)
        cp = pltpu.make_async_remote_copy(
            acc.at[q], accin.at[t], tss.at[t], trs.at[t], device_id=(i, q), device_id_type=MESH
        )
        cp.start()
        lasts.append(cp)
    final = acc[j]
    for t in range(1, NSTA):
        lasts[t - 1].wait_recv()
        final = final + accin[t]
    out[...] = final
    for cp in halos + asks + msgs + sums + lasts:
        cp.wait_send()


def on_device(model_change, sens_blocks, block_rows, block_cols, live_count, owner_order):
    anyspace = pl.BlockSpec(memory_space=pl.ANY)
    dma = pltpu.SemaphoreType.DMA
    vm = pltpu.VMEM
    return pl.pallas_call(
        kernel,
        out_shape=jax.ShapeDtypeStruct((EP, BLK), F32),
        in_specs=[anyspace] * 7,
        out_specs=pl.BlockSpec(memory_space=pltpu.VMEM),
        scratch_shapes=[
            vm((EP, SX, SY, NZ), F32), vm((K, BLK, BLK), BF16), vm((3 * NZ, NZ), BF16),
            vm((1, K), I32), vm((1, K), I32), vm((1, BLK), I32), pltpu.SMEM((1, 1), I32),
            vm((EP, SY, NZ), F32), vm((SX * 4, NZ), F32), vm((8, NZ), F32),
            vm((EP, SY, NZ), F32), vm((SX * 4, NZ), F32), vm((8, NZ), F32),
            vm((2, SX, SY * 4 + 8, BLK), F32), vm((CB * 4, BLK), F32),
            vm((CAP // 8, 32, BLK), F32), vm((NSLAB, MSG, BLK), BF16), vm((NSLAB, MSG, BLK), BF16),
            vm((NSLAB * MSG, BLK), F32), vm((MSG // 2, BLK), F32), vm((K * 4, BLK), F32), vm((BLK, K), BF16),
            vm((NSLAB, 1, BLK), I32), vm((NSLAB, 1, BLK), I32), pltpu.SMEM((NSLAB, 1, BLK), I32),
            vm((2, K), I32), pltpu.SMEM((2, K), I32),
            vm((BLK * 4, BLK), F32), vm((NSLAB, 32, BLK), F32),
            vm((NSTA, 4, BLK), F32), vm((NSTA, 4, BLK), F32),
            dma((9,)), dma((3,)), dma((3,)), dma((NSLAB,)), dma((NSLAB,)), dma((NSLAB,)), dma((NSLAB,)),
            dma((NSLAB,)), dma((NSLAB,)), dma((NSTA,)), dma((NSTA,)),
        ],
        compiler_params=pltpu.CompilerParams(
            collective_id=0, has_side_effects=True, vmem_limit_bytes=52 * 2**20
        ),
        name="gravity_step",
    )(
        model_change,
        sens_blocks.reshape(K, BLK, BLK),
        block_cols.reshape(1, K),
        block_rows.reshape(1, K),
        live_count.reshape(1, 1),
        owner_order.reshape(1, BLK),
        jnp.asarray(z_matrix()),
    )


def solution(mesh):
    placed = (
        P(None, "slab", "sta", None),
        P("slab", "sta", None, None, None),
        P("slab", "sta", None),
        P("slab", "sta", None),
        P("slab", "sta"),
        P(),
    )
    return jax.shard_map(
        on_device, mesh=mesh, in_specs=placed, out_specs=P(None, ("slab", "sta")), check_vma=False
    )
```

```python
import functools
import math

import jax
import jax.numpy as jnp
import ml_dtypes
import numpy as np
from jax import lax
from jax.experimental import pallas as pl
from jax.experimental.pallas import tpu as pltpu
from jax.sharding import PartitionSpec as P

MESH = pl.DeviceIdType.MESH
F32, BF16, I32 = jnp.float32, jnp.bfloat16, jnp.int32
NT = (((1,), (1,)), ((), ()))
R3 = math.sqrt(3.0)
H0, H1, H2, H3 = (
    (1.0 + R3) / (4.0 * math.sqrt(2.0)),
    (3.0 + R3) / (4.0 * math.sqrt(2.0)),
    (3.0 - R3) / (4.0 * math.sqrt(2.0)),
    (1.0 - R3) / (4.0 * math.sqrt(2.0)),
)
C1, C2 = H3 / H0, H1 / H2

EP, SX, SY, NZ, BLK = 4, 12, 32, 256, 128
K, CAP, CB = 640, 80, 768
NSLAB, NSTA = 16, 8
MSG = CAP * EP
KT = K // BLK
NDEV = NSLAB * NSTA
SLICES = ((0, 24), (24, 48), (48, 64), (64, 80))
GROUP = 32


def torus(step):
    dx, dz = divmod(step, 4)
    return min(dx, 4 - dx) + min(dz, 4 - dz)


STEPS = [(0, 0)] + [divmod(s, 4) for s in sorted(range(1, 16), key=lambda s: -torus(s))]


def z_matrix():
    w = np.zeros((NZ, NZ), np.float64)
    for k in range(NZ // 2):
        src = [(2 * k + d) % NZ for d in range(4)]
        for at, lo, hi in zip(src, (H0, H1, H2, H3), (H3, -H2, H1, -H0)):
            w[at, 2 * k] = lo
            w[at, 2 * k + 1] = hi
    top = w.astype(ml_dtypes.bfloat16)
    rest = (w - top.astype(np.float64)).astype(ml_dtypes.bfloat16)
    return np.concatenate([top, top, rest], 0)


def kernel(
    model, sens, cols, rows, live, owner, wz, out,
    X, sv, wv, cv, rv, ov, lv, Sx, Sy, Sc, Rx, Ry, Rc, D, C, st, send, recv, work, gat, T, R,
    reqv, reqin, reqs, lists, lists_s, red, outs, ins,
    lsem, hss, hrs, qss, qrs, ass_, ars, rss, rrs,
):
    i, j = lax.axis_index("slab"), lax.axis_index("sta")
    xx, zz = i // 4, lax.rem(i, 4)

    loads = [
        pltpu.make_async_copy(src, dst, lsem.at[n])
        for n, (src, dst) in enumerate(
            ((cols, cv), (rows, rv), (owner, ov), (live, lv), (model, X), (wz, wv), (sens, sv))
        )
    ]
    for cp in loads:
        cp.start()

    def ahead(n):
        dx, dz = STEPS[n]
        return lax.rem(xx + dx, 4) * 4 + lax.rem(zz + dz, 4)

    def behind(n):
        dx, dz = STEPS[n]
        return lax.rem(xx + 4 - dx, 4) * 4 + lax.rem(zz + 4 - dz, 4)

    up_i, down_i = lax.rem(i + 1, NSLAB), lax.rem(i + NSLAB - 1, NSLAB)
    up_j, down_j = lax.rem(j + 1, NSTA), lax.rem(j + NSTA - 1, NSTA)

    bar = pltpu.get_barrier_semaphore()
    for n in range(1, NSLAB):
        pl.semaphore_signal(bar, inc=1, device_id=(ahead(n), j), device_id_type=MESH)
    for t in range(1, NSTA):
        pl.semaphore_signal(bar, inc=1, device_id=(i, lax.rem(j + t, NSTA)), device_id_type=MESH)
    pl.semaphore_signal(bar, inc=1, device_id=(up_i, up_j), device_id_type=MESH)

    for cp in loads[:4]:
        cp.wait()
    sub16 = lax.broadcasted_iota(I32, (16, BLK), 0)
    sub128 = lax.broadcasted_iota(I32, (BLK, BLK), 0)
    lane128 = lax.broadcasted_iota(I32, (BLK, BLK), 1)
    sub8 = lax.broadcasted_iota(I32, (8, BLK), 0)
    lane8 = lax.broadcasted_iota(I32, (8, BLK), 1)
    one = lambda m: jnp.where(m, 1.0, 0.0).astype(BF16)
    peer = jnp.zeros((16, BLK), I32)
    for n in range(NSLAB):
        peer = jnp.where(sub16 == n, behind(n), peer)
    first = peer * CB
    upper = one(sub128 < lane128)
    ties, ranks, rels = [], [], []
    carry = jnp.zeros((16, 1), F32)
    for t in range(KT):
        rel = cv[:, t * BLK : (t + 1) * BLK] - first
        tie = (rel >= 0) & (rel < CB)
        tie_f = jnp.where(tie, 1.0, 0.0)
        ranks.append(jnp.dot(tie_f.astype(BF16), upper, preferred_element_type=F32) + carry)
        carry = carry + jnp.sum(tie_f, axis=1, keepdims=True)
        ties.append(tie_f)
        rels.append(jnp.where(tie, rel, 0))
    count = jnp.broadcast_to(carry, (16, BLK))
    bases = []
    for lo, hi in SLICES:
        inside = jnp.clip(count - lo, 0.0, hi - lo)
        scan = inside
        for s in (1, 2, 4, 8):
            scan = scan + jnp.where(sub16 >= s, pltpu.roll(scan, s, 0), 0.0)
        before = jnp.sum(jnp.minimum(count, lo), axis=0, keepdims=True)
        bases.append(before + scan - inside - lo)

    place = one(sub128 == ov[...])
    inverse = lax.dot_general(
        lane8.astype(F32).astype(BF16), place, NT, preferred_element_type=F32
    ).astype(BF16)
    live_now = lv[0, 0]
    ask = jnp.zeros((32, BLK), F32)
    vals, spots = [], []
    for t in range(KT):
        rank_k = jnp.sum(ties[t] * ranks[t], axis=0, keepdims=True).astype(I32)
        slot_k = jnp.sum(ties[t] * (jnp.minimum(ranks[t], CAP - 1.0) + sub16.astype(F32) * CAP), axis=0, keepdims=True).astype(I32)
        base = bases[0]
        for (lo, _), later in zip(SLICES[1:], bases[1:]):
            base = jnp.where(ranks[t] >= lo, later, base)
        spots.append(jnp.sum(ties[t] * (ranks[t] + base), axis=0, keepdims=True).astype(I32))
        rel = rels[t]
        cell = (rel & -64) + ((rel & 1) << 5) + ((rel >> 1) & 31)
        pair = jnp.concatenate([(cell >> 3).astype(F32), (cell & 7).astype(F32)], 0).astype(BF16)
        ask = ask + lax.dot_general(pair, one(sub128 == rank_k), NT, preferred_element_type=F32)
        dest = jnp.dot(
            inverse, one(sub128 == rv[:, t * BLK : (t + 1) * BLK]), preferred_element_type=F32
        )
        here = lane8 + t * BLK
        dest = jnp.where(here < live_now, dest, 128.0)
        slot8 = jnp.broadcast_to(slot_k, (8, BLK))
        val = jnp.where(sub8 == 0, here >> 3, here & 7)
        val = jnp.where(sub8 == 2, slot8 >> 3, val)
        val = jnp.where(sub8 == 3, slot8 & 7, val).astype(F32)
        vals.append(jnp.where(sub8 == 4, dest, val).astype(BF16))
    ask = jnp.clip((ask[:16] * 8.0 + ask[16:]).astype(I32), 0, CB - 1)
    for n in range(NSLAB):
        if n == 0:
            reqin[n] = ask[n : n + 1]
        else:
            reqv[n] = ask[n : n + 1]

    loads[4].wait()
    for e in range(EP):
        Sx[e] = H2 * X[e, 0] + H3 * X[e, 1]
    for e in range(EP):
        for x in range(SX):
            Sy[4 * x + e : 4 * x + e + 1, :] = H2 * X[e, x, 0:1, :] + H3 * X[e, x, 1:2, :]
    Sc[0:4, :] = H2 * Sy[0:4, :] + H3 * Sy[4:8, :]
    Sc[4:8, :] = jnp.zeros((4, NZ), F32)

    pl.semaphore_wait(bar, NSLAB - 1 + NSTA - 1 + 1)
    halos = [
        pltpu.make_async_remote_copy(src, dst, hss.at[n], hrs.at[n], device_id=dev, device_id_type=MESH)
        for n, (src, dst, dev) in enumerate(
            ((Sy, Ry, (i, down_j)), (Sc, Rc, (down_i, down_j)), (Sx, Rx, (down_i, j)))
        )
    ]
    for cp in halos:
        cp.start()
    asks = [
        pltpu.make_async_remote_copy(
            reqv.at[n], reqin.at[n], qss.at[n], qrs.at[n], device_id=(behind(n), j), device_id_type=MESH
        )
        for n in range(1, NSLAB)
    ]
    for cp in asks:
        cp.start()

    def spread(x, e, q, val):
        for z in range(2):
            D[z, x, pl.ds(32 * q + e, 8, stride=4), :] = val[:, z * BLK : (z + 1) * BLK]

    def x_pair(k, _):
        for e in range(EP):
            for q in range(SY // 8):
                at = slice(8 * q, 8 * q + 8)
                s = H0 * X[e, 2 * k, at, :] + H1 * X[e, 2 * k + 1, at, :]
                t = H2 * X[e, 2 * k + 2, at, :] + H3 * X[e, 2 * k + 3, at, :]
                spread(2 * k, e, q, s + t)
                spread(2 * k + 1, e, q, C1 * s + C2 * t)
        return 0

    lax.fori_loop(0, SX // 2 - 1, x_pair, 0)

    order = []
    for u in range(KT):
        got = jnp.zeros((8, BLK), F32)
        for t in range(KT):
            got = got + lax.dot_general(
                vals[t], one(sub128 + u * BLK == spots[t]), NT, preferred_element_type=F32
            )
        dest = got[4:5].astype(I32)
        R[:, u * BLK : (u + 1) * BLK] = one(sub128 == dest)
        lists[0:1, u * BLK : (u + 1) * BLK] = jnp.clip(
            (got[0:1] * 8.0 + got[1:2]).astype(I32), 0, K - 1
        )
        lists[1:2, u * BLK : (u + 1) * BLK] = jnp.clip(
            (got[2:3] * 8.0 + got[3:4]).astype(I32), 0, NSLAB * CAP - 1
        )
    to_s = pltpu.make_async_copy(lists, lists_s, lsem.at[7])
    to_s.start()

    low = lax.broadcasted_iota(I32, (8, BLK), 0) < 4
    ca, cb = jnp.where(low, H0, -H2), jnp.where(low, H1, H3)
    cc, cd = jnp.where(low, H2, -H0), jnp.where(low, H3, H1)
    ce = jnp.where(lax.broadcasted_iota(I32, (8, NZ), 0) < 4, 1.0, C2)
    loads[5].wait()

    def y_inner(x):
        parts = []
        for z in range(2):
            v = D[z, x].reshape(SY // 2, 8, BLK)
            u = pltpu.roll(v, 4, 1)
            t = cc * v[1:] + cd * u[1:]
            none = jnp.zeros((1, 8, BLK), F32)
            parts.append((ca * v + cb * u + jnp.concatenate([t, none], 0)).reshape(SY * 4, BLK))
        return jnp.concatenate(parts, 1)

    def z_pass(full):
        high = full.astype(BF16)
        rest = (full - high.astype(F32)).astype(BF16)
        return jnp.dot(jnp.concatenate([high, rest, high], 1), wv[...], preferred_element_type=F32)

    def yz(x, _):
        res = z_pass(y_inner(x))
        at = pl.multiple_of(x * 2 * SY * 4, 2 * SY * 4)
        C[pl.ds(at, SY * 4), :] = res[:, :BLK]
        C[pl.ds(at + SY * 4, SY * 4), :] = res[:, BLK:]
        return 0

    lax.fori_loop(0, SX - 2, yz, 0)

    for cp in halos:
        cp.wait_recv()
    for e in range(EP):
        for q in range(SY // 8):
            at = slice(8 * q, 8 * q + 8)
            s = H0 * X[e, SX - 2, at, :] + H1 * X[e, SX - 1, at, :]
            t = Rx[e, at, :]
            spread(SX - 2, e, q, s + t)
            spread(SX - 1, e, q, C1 * s + C2 * t)
    lax.fori_loop(SX - 2, SX, yz, 0)
    rims = []
    for k in range(SX // 2):
        s = H0 * Ry[8 * k : 8 * k + 4, :] + H1 * Ry[8 * k + 4 : 8 * k + 8, :]
        if k < SX // 2 - 1:
            t = H2 * Ry[8 * k + 8 : 8 * k + 12, :] + H3 * Ry[8 * k + 12 : 8 * k + 16, :]
        else:
            t = Rc[0:4, :]
        for rim in (s + t, C1 * s + C2 * t):
            rims.append(ce * jnp.concatenate([rim, rim], 0))
    added = z_pass(jnp.concatenate(rims, 0))
    for x in range(SX):
        for z in range(2):
            at = (2 * x + z + 1) * SY * 4 - 8
            C[at : at + 8, :] = C[at : at + 8, :] + added[8 * x : 8 * x + 8, z * BLK : (z + 1) * BLK]

    for cp in asks:
        cp.wait_recv()
    to_r = pltpu.make_async_copy(reqin, reqs, lsem.at[8])
    to_r.start()
    to_r.wait()
    to_s.wait()

    def pack(n, lo, hi):
        def some(g, _):
            for a in range(8):
                c = reqs[n, 0, g * 8 + a]
                st[g, 4 * a : 4 * a + 4, :] = C[pl.ds(c * 4, 4), :]
            return 0

        lax.fori_loop(lo // 8, hi // 8, some, 0)
        return st[lo // 8 : hi // 8].reshape((hi - lo) * 4, BLK).astype(BF16)

    msgs = {}
    for m, (lo, hi) in enumerate(SLICES):
        at = pl.ds(4 * lo, 4 * (hi - lo))
        for n in range(1, NSLAB):
            send[n, at, :] = pack(n, lo, hi)
            sem = m * NSLAB + n
            msgs[m, n] = pltpu.make_async_remote_copy(
                send.at[n, at, :], recv.at[n, at, :], ass_.at[sem], ars.at[sem],
                device_id=(ahead(n), j), device_id_type=MESH,
            )
            msgs[m, n].start()
    work[0:MSG, :] = pack(0, 0, CAP).astype(F32)

    loads[6].wait()
    first_half = lax.broadcasted_iota(I32, (8, BLK), 0) < 4

    def products(g, _):
        for a in range(GROUP):
            c = lists_s[1, g * GROUP + a]
            gat[4 * a : 4 * a + 4, :] = work[pl.ds(c * 4, 4), :]
        for a in range(0, GROUP, 2):
            lhs = gat[4 * a : 4 * a + 8, :].astype(BF16)
            rhs = jnp.concatenate([sv[lists_s[0, g * GROUP + a]], sv[lists_s[0, g * GROUP + a + 1]]], 0)
            res = lax.dot_general(lhs, rhs, NT, preferred_element_type=F32)
            at = pl.multiple_of(g * GROUP * 4, GROUP * 4) + 4 * a
            T[pl.ds(at, 8), :] = jnp.where(first_half, res[:, :BLK], res[:, BLK:])
        return 0

    def route(lo, hi):
        sums = []
        for e in range(EP):
            term = T[pl.ds(lo * 4 + e, hi - lo, stride=4), :]
            high = term.astype(BF16)
            rest = (term - high.astype(F32)).astype(BF16)
            r = R[:, lo:hi]
            sums.append(
                jnp.dot(r, high, preferred_element_type=F32) + jnp.dot(r, rest, preferred_element_type=F32)
            )
        return sums

    for m, (lo, hi) in enumerate(SLICES):
        for n in range(1, NSLAB):
            msgs[m, n].wait_recv()
            work[n * MSG + 4 * lo : n * MSG + 4 * hi, :] = recv[n, 4 * lo : 4 * hi, :].astype(F32)
        lax.fori_loop(8 * lo // GROUP, 8 * hi // GROUP, products, 0)
        if hi == 64:
            for e, part in enumerate(route(0, 512)):
                red[pl.ds(e, BLK, stride=4), :] = part
    for e, part in enumerate(route(512, K)):
        red[pl.ds(e, BLK, stride=4), :] = red[pl.ds(e, BLK, stride=4), :] + part
    for b in range(NDEV):
        outs[b] = red[4 * b : 4 * b + 4, :]

    me = i * NSTA + j

    def give(t, _):
        d = lax.rem(me + t, NDEV)
        pltpu.make_async_remote_copy(
            outs.at[d], ins.at[me], rss.at[0], rrs.at[0],
            device_id=(d // NSTA, lax.rem(d, NSTA)), device_id_type=MESH,
        ).start()
        return 0

    lax.fori_loop(1, NDEV, give, 0)
    ins[me] = outs[me]
    rest = pl.ds(0, NDEV - 1)
    every = pltpu.make_async_remote_copy(
        outs.at[rest], ins.at[rest], rss.at[0], rrs.at[0], device_id=(i, j), device_id_type=MESH
    )
    every.wait_recv()
    out[...] = jnp.sum(jnp.sum(ins[...].reshape(8, NDEV // 8, 4, BLK), axis=1), axis=0)
    every.wait_send()
    for cp in halos + asks + list(msgs.values()):
        cp.wait_send()


def on_device(model_change, sens_blocks, block_rows, block_cols, live_count, owner_order):
    anyspace = pl.BlockSpec(memory_space=pl.ANY)
    dma = pltpu.SemaphoreType.DMA
    vm = pltpu.VMEM
    return pl.pallas_call(
        kernel,
        out_shape=jax.ShapeDtypeStruct((EP, BLK), F32),
        in_specs=[anyspace] * 7,
        out_specs=pl.BlockSpec(memory_space=pltpu.VMEM),
        scratch_shapes=[
            vm((EP, SX, SY, NZ), F32), vm((K, BLK, BLK), BF16), vm((3 * NZ, NZ), BF16),
            vm((1, K), I32), vm((1, K), I32), vm((1, BLK), I32), pltpu.SMEM((1, 1), I32),
            vm((EP, SY, NZ), F32), vm((SX * 4, NZ), F32), vm((8, NZ), F32),
            vm((EP, SY, NZ), F32), vm((SX * 4, NZ), F32), vm((8, NZ), F32),
            vm((2, SX, SY * 4, BLK), F32), vm((CB * 4, BLK), F32),
            vm((CAP // 8, 32, BLK), F32), vm((NSLAB, MSG, BLK), BF16), vm((NSLAB, MSG, BLK), BF16),
            vm((NSLAB * MSG, BLK), F32), vm((GROUP * 4, BLK), F32), vm((K * 4, BLK), F32), vm((BLK, K), BF16),
            vm((NSLAB, 1, BLK), I32), vm((NSLAB, 1, BLK), I32), pltpu.SMEM((NSLAB, 1, BLK), I32),
            vm((2, K), I32), pltpu.SMEM((2, K), I32),
            vm((BLK * 4, BLK), F32), vm((NDEV, 4, BLK), F32), vm((NDEV, 4, BLK), F32),
            dma((9,)), dma((3,)), dma((3,)), dma((NSLAB,)), dma((NSLAB,)),
            dma((4 * NSLAB,)), dma((4 * NSLAB,)), dma((1,)), dma((1,)),
        ],
        compiler_params=pltpu.CompilerParams(
            collective_id=0, has_side_effects=True, vmem_limit_bytes=60 * 2**20
        ),
        name="gravity_step",
    )(
        model_change,
        sens_blocks.reshape(K, BLK, BLK),
        block_cols.reshape(1, K),
        block_rows.reshape(1, K),
        live_count.reshape(1, 1),
        owner_order.reshape(1, BLK),
        jnp.asarray(z_matrix()),
    )


def solution(mesh):
    placed = (
        P(None, "slab", "sta", None),
        P("slab", "sta", None, None, None),
        P("slab", "sta", None),
        P("slab", "sta", None),
        P("slab", "sta"),
        P(),
    )
    return jax.shard_map(
        on_device, mesh=mesh, in_specs=placed, out_specs=P(None, ("slab", "sta")), check_vma=False
    )
```

```python
import functools
import math

import jax
import jax.numpy as jnp
import ml_dtypes
import numpy as np
from jax import lax
from jax.experimental import pallas as pl
from jax.experimental.pallas import tpu as pltpu
from jax.sharding import PartitionSpec as P

MESH = pl.DeviceIdType.MESH
F32, BF16, I32 = jnp.float32, jnp.bfloat16, jnp.int32
NT = (((1,), (1,)), ((), ()))
R3 = math.sqrt(3.0)
H0, H1, H2, H3 = (
    (1.0 + R3) / (4.0 * math.sqrt(2.0)),
    (3.0 + R3) / (4.0 * math.sqrt(2.0)),
    (3.0 - R3) / (4.0 * math.sqrt(2.0)),
    (1.0 - R3) / (4.0 * math.sqrt(2.0)),
)
C1, C2 = H3 / H0, H1 / H2

EP, SX, SY, NZ, BLK = 4, 12, 32, 256, 128
K, CAP, CB = 640, 80, 768
NSLAB, NSTA = 16, 8
MSG = CAP * EP
KT = K // BLK
NDEV = NSLAB * NSTA
SLICES = ((0, 24), (24, 48), (48, 64), (64, 80))
GROUP = 32


def torus(step):
    dx, dz = divmod(step, 4)
    return min(dx, 4 - dx) + min(dz, 4 - dz)


STEPS = [(0, 0), (2, 2), (1, 2), (3, 2), (2, 1), (2, 3), (1, 1), (3, 3), (1, 3), (3, 1), (2, 0), (0, 2), (1, 0), (0, 1), (3, 0), (0, 3)]


def z_matrix():
    w = np.zeros((NZ, NZ), np.float64)
    for k in range(NZ // 2):
        src = [(2 * k + d) % NZ for d in range(4)]
        for at, lo, hi in zip(src, (H0, H1, H2, H3), (H3, -H2, H1, -H0)):
            w[at, 2 * k] = lo
            w[at, 2 * k + 1] = hi
    top = w.astype(ml_dtypes.bfloat16)
    rest = (w - top.astype(np.float64)).astype(ml_dtypes.bfloat16)
    return np.concatenate([top, top, rest], 0)


def kernel(
    model, sens, cols, rows, live, owner, wz, out,
    X, sv, wv, cv, rv, ov, lv, Sx, Sy, Sc, Rx, Ry, Rc, D, C, st, send, recv, work, gat, T, R,
    reqv, reqin, reqs, lists, lists_s, red, outs, ins,
    lsem, hss, hrs, qss, qrs, ass_, ars, rss, rrs,
):
    i, j = lax.axis_index("slab"), lax.axis_index("sta")
    xx, zz = i // 4, lax.rem(i, 4)

    loads = [
        pltpu.make_async_copy(src, dst, lsem.at[n])
        for n, (src, dst) in enumerate(
            ((cols, cv), (rows, rv), (owner, ov), (live, lv), (model, X), (wz, wv), (sens, sv))
        )
    ]
    for cp in loads:
        cp.start()

    core = lax.rem(j, 2)

    def partner(n, sign):
        dx, dz = ((sign * d) % 4 for d in STEPS[n])
        mx, mz = (1 * dz) % 4, (1 * dx) % 4
        ax = dx + core * (mx - dx)
        az = dz + core * (mz - dz)
        return lax.rem(xx + ax, 4) * 4 + lax.rem(zz + az, 4)

    ahead = functools.partial(partner, sign=1)
    behind = functools.partial(partner, sign=-1)

    up_i, down_i = lax.rem(i + 1, NSLAB), lax.rem(i + NSLAB - 1, NSLAB)
    up_j, down_j = lax.rem(j + 1, NSTA), lax.rem(j + NSTA - 1, NSTA)

    bar = pltpu.get_barrier_semaphore()
    for n in range(1, NSLAB):
        pl.semaphore_signal(bar, inc=1, device_id=(ahead(n), j), device_id_type=MESH)
    for t in range(1, NSTA):
        pl.semaphore_signal(bar, inc=1, device_id=(i, lax.rem(j + t, NSTA)), device_id_type=MESH)
    pl.semaphore_signal(bar, inc=1, device_id=(up_i, up_j), device_id_type=MESH)

    for cp in loads[:4]:
        cp.wait()
    sub16 = lax.broadcasted_iota(I32, (16, BLK), 0)
    sub128 = lax.broadcasted_iota(I32, (BLK, BLK), 0)
    lane128 = lax.broadcasted_iota(I32, (BLK, BLK), 1)
    sub8 = lax.broadcasted_iota(I32, (8, BLK), 0)
    lane8 = lax.broadcasted_iota(I32, (8, BLK), 1)
    one = lambda m: jnp.where(m, 1.0, 0.0).astype(BF16)
    peer = jnp.zeros((16, BLK), I32)
    for n in range(NSLAB):
        peer = jnp.where(sub16 == n, behind(n), peer)
    first = peer * CB
    upper = one(sub128 < lane128)
    ties, ranks, rels = [], [], []
    carry = jnp.zeros((16, 1), F32)
    for t in range(KT):
        rel = cv[:, t * BLK : (t + 1) * BLK] - first
        tie = (rel >= 0) & (rel < CB)
        tie_f = jnp.where(tie, 1.0, 0.0)
        ranks.append(jnp.dot(tie_f.astype(BF16), upper, preferred_element_type=F32) + carry)
        carry = carry + jnp.sum(tie_f, axis=1, keepdims=True)
        ties.append(tie_f)
        rels.append(jnp.where(tie, rel, 0))
    count = jnp.broadcast_to(carry, (16, BLK))
    bases = []
    for lo, hi in SLICES:
        inside = jnp.clip(count - lo, 0.0, hi - lo)
        scan = inside
        for s in (1, 2, 4, 8):
            scan = scan + jnp.where(sub16 >= s, pltpu.roll(scan, s, 0), 0.0)
        before = jnp.sum(jnp.minimum(count, lo), axis=0, keepdims=True)
        bases.append(before + scan - inside - lo)

    place = one(sub128 == ov[...])
    inverse = lax.dot_general(
        lane8.astype(F32).astype(BF16), place, NT, preferred_element_type=F32
    ).astype(BF16)
    live_now = lv[0, 0]
    ask = jnp.zeros((32, BLK), F32)
    vals, spots = [], []
    for t in range(KT):
        rank_k = jnp.sum(ties[t] * ranks[t], axis=0, keepdims=True).astype(I32)
        slot_k = jnp.sum(ties[t] * (jnp.minimum(ranks[t], CAP - 1.0) + sub16.astype(F32) * CAP), axis=0, keepdims=True).astype(I32)
        base = bases[0]
        for (lo, _), later in zip(SLICES[1:], bases[1:]):
            base = jnp.where(ranks[t] >= lo, later, base)
        spots.append(jnp.sum(ties[t] * (ranks[t] + base), axis=0, keepdims=True).astype(I32))
        rel = rels[t]
        cell = (rel & -64) + ((rel & 1) << 5) + ((rel >> 1) & 31)
        pair = jnp.concatenate([(cell >> 3).astype(F32), (cell & 7).astype(F32)], 0).astype(BF16)
        ask = ask + lax.dot_general(pair, one(sub128 == rank_k), NT, preferred_element_type=F32)
        dest = jnp.dot(
            inverse, one(sub128 == rv[:, t * BLK : (t + 1) * BLK]), preferred_element_type=F32
        )
        here = lane8 + t * BLK
        dest = jnp.where(here < live_now, dest, 128.0)
        slot8 = jnp.broadcast_to(slot_k, (8, BLK))
        val = jnp.where(sub8 == 0, here >> 3, here & 7)
        val = jnp.where(sub8 == 2, slot8 >> 3, val)
        val = jnp.where(sub8 == 3, slot8 & 7, val).astype(F32)
        vals.append(jnp.where(sub8 == 4, dest, val).astype(BF16))
    ask = jnp.clip((ask[:16] * 8.0 + ask[16:]).astype(I32), 0, CB - 1)
    for n in range(NSLAB):
        if n == 0:
            reqin[n] = ask[n : n + 1]
        else:
            reqv[n] = ask[n : n + 1]

    loads[4].wait()
    for e in range(EP):
        Sx[e] = H2 * X[e, 0] + H3 * X[e, 1]
    for e in range(EP):
        for x in range(SX):
            Sy[4 * x + e : 4 * x + e + 1, :] = H2 * X[e, x, 0:1, :] + H3 * X[e, x, 1:2, :]
    Sc[0:4, :] = H2 * Sy[0:4, :] + H3 * Sy[4:8, :]
    Sc[4:8, :] = jnp.zeros((4, NZ), F32)

    pl.semaphore_wait(bar, NSLAB - 1 + NSTA - 1 + 1)
    halos = [
        pltpu.make_async_remote_copy(src, dst, hss.at[n], hrs.at[n], device_id=dev, device_id_type=MESH)
        for n, (src, dst, dev) in enumerate(
            ((Sy, Ry, (i, down_j)), (Sc, Rc, (down_i, down_j)), (Sx, Rx, (down_i, j)))
        )
    ]
    for cp in halos:
        cp.start()
    asks = [
        pltpu.make_async_remote_copy(
            reqv.at[n], reqin.at[n], qss.at[n], qrs.at[n], device_id=(behind(n), j), device_id_type=MESH
        )
        for n in range(1, NSLAB)
    ]
    for cp in asks:
        cp.start()

    def spread(x, e, q, val):
        for z in range(2):
            D[z, x, pl.ds(32 * q + e, 8, stride=4), :] = val[:, z * BLK : (z + 1) * BLK]

    def x_pair(k, _):
        for e in range(EP):
            for q in range(SY // 8):
                at = slice(8 * q, 8 * q + 8)
                s = H0 * X[e, 2 * k, at, :] + H1 * X[e, 2 * k + 1, at, :]
                t = H2 * X[e, 2 * k + 2, at, :] + H3 * X[e, 2 * k + 3, at, :]
                spread(2 * k, e, q, s + t)
                spread(2 * k + 1, e, q, C1 * s + C2 * t)
        return 0

    lax.fori_loop(0, SX // 2 - 1, x_pair, 0)

    order = []
    for u in range(KT):
        got = jnp.zeros((8, BLK), F32)
        for t in range(KT):
            got = got + lax.dot_general(
                vals[t], one(sub128 + u * BLK == spots[t]), NT, preferred_element_type=F32
            )
        dest = got[4:5].astype(I32)
        R[:, u * BLK : (u + 1) * BLK] = one(sub128 == dest)
        lists[0:1, u * BLK : (u + 1) * BLK] = jnp.clip(
            (got[0:1] * 8.0 + got[1:2]).astype(I32), 0, K - 1
        )
        lists[1:2, u * BLK : (u + 1) * BLK] = jnp.clip(
            (got[2:3] * 8.0 + got[3:4]).astype(I32), 0, NSLAB * CAP - 1
        )
    to_s = pltpu.make_async_copy(lists, lists_s, lsem.at[7])
    to_s.start()

    low = lax.broadcasted_iota(I32, (8, BLK), 0) < 4
    ca, cb = jnp.where(low, H0, -H2), jnp.where(low, H1, H3)
    cc, cd = jnp.where(low, H2, -H0), jnp.where(low, H3, H1)
    ce = jnp.where(lax.broadcasted_iota(I32, (8, NZ), 0) < 4, 1.0, C2)
    loads[5].wait()

    def y_inner(x):
        parts = []
        for z in range(2):
            v = D[z, x].reshape(SY // 2, 8, BLK)
            u = pltpu.roll(v, 4, 1)
            t = cc * v[1:] + cd * u[1:]
            none = jnp.zeros((1, 8, BLK), F32)
            parts.append((ca * v + cb * u + jnp.concatenate([t, none], 0)).reshape(SY * 4, BLK))
        return jnp.concatenate(parts, 1)

    def z_pass(full):
        high = full.astype(BF16)
        rest = (full - high.astype(F32)).astype(BF16)
        return jnp.dot(jnp.concatenate([high, rest, high], 1), wv[...], preferred_element_type=F32)

    def yz(x, _):
        res = z_pass(y_inner(x))
        at = pl.multiple_of(x * 2 * SY * 4, 2 * SY * 4)
        C[pl.ds(at, SY * 4), :] = res[:, :BLK]
        C[pl.ds(at + SY * 4, SY * 4), :] = res[:, BLK:]
        return 0

    lax.fori_loop(0, SX - 2, yz, 0)

    for cp in halos:
        cp.wait_recv()
    for e in range(EP):
        for q in range(SY // 8):
            at = slice(8 * q, 8 * q + 8)
            s = H0 * X[e, SX - 2, at, :] + H1 * X[e, SX - 1, at, :]
            t = Rx[e, at, :]
            spread(SX - 2, e, q, s + t)
            spread(SX - 1, e, q, C1 * s + C2 * t)
    lax.fori_loop(SX - 2, SX, yz, 0)
    rims = []
    for k in range(SX // 2):
        s = H0 * Ry[8 * k : 8 * k + 4, :] + H1 * Ry[8 * k + 4 : 8 * k + 8, :]
        if k < SX // 2 - 1:
            t = H2 * Ry[8 * k + 8 : 8 * k + 12, :] + H3 * Ry[8 * k + 12 : 8 * k + 16, :]
        else:
            t = Rc[0:4, :]
        for rim in (s + t, C1 * s + C2 * t):
            rims.append(ce * jnp.concatenate([rim, rim], 0))
    added = z_pass(jnp.concatenate(rims, 0))
    for x in range(SX):
        for z in range(2):
            at = (2 * x + z + 1) * SY * 4 - 8
            C[at : at + 8, :] = C[at : at + 8, :] + added[8 * x : 8 * x + 8, z * BLK : (z + 1) * BLK]

    for cp in asks:
        cp.wait_recv()
    to_r = pltpu.make_async_copy(reqin, reqs, lsem.at[8])
    to_r.start()
    to_r.wait()
    to_s.wait()

    def pack(n, lo, hi):
        def some(g, _):
            for a in range(8):
                c = reqs[n, 0, g * 8 + a]
                st[g, 4 * a : 4 * a + 4, :] = C[pl.ds(c * 4, 4), :]
            return 0

        lax.fori_loop(lo // 8, hi // 8, some, 0)
        return st[lo // 8 : hi // 8].reshape((hi - lo) * 4, BLK).astype(BF16)

    msgs = {}
    for m, (lo, hi) in enumerate(SLICES):
        at = pl.ds(4 * lo, 4 * (hi - lo))
        for n in range(1, NSLAB):
            send[n, at, :] = pack(n, lo, hi)
            sem = m * NSLAB + n
            msgs[m, n] = pltpu.make_async_remote_copy(
                send.at[n, at, :], recv.at[n, at, :], ass_.at[sem], ars.at[sem],
                device_id=(ahead(n), j), device_id_type=MESH,
            )
            msgs[m, n].start()
    work[0:MSG, :] = pack(0, 0, CAP).astype(F32)

    loads[6].wait()
    first_half = lax.broadcasted_iota(I32, (8, BLK), 0) < 4

    def products(g, _):
        for a in range(GROUP):
            c = lists_s[1, g * GROUP + a]
            gat[4 * a : 4 * a + 4, :] = work[pl.ds(c * 4, 4), :]
        for a in range(0, GROUP, 2):
            lhs = gat[4 * a : 4 * a + 8, :].astype(BF16)
            rhs = jnp.concatenate([sv[lists_s[0, g * GROUP + a]], sv[lists_s[0, g * GROUP + a + 1]]], 0)
            res = lax.dot_general(lhs, rhs, NT, preferred_element_type=F32)
            at = pl.multiple_of(g * GROUP * 4, GROUP * 4) + 4 * a
            T[pl.ds(at, 8), :] = jnp.where(first_half, res[:, :BLK], res[:, BLK:])
        return 0

    def route(lo, hi):
        sums = []
        for e in range(EP):
            term = T[pl.ds(lo * 4 + e, hi - lo, stride=4), :]
            high = term.astype(BF16)
            rest = (term - high.astype(F32)).astype(BF16)
            r = R[:, lo:hi]
            sums.append(
                jnp.dot(r, high, preferred_element_type=F32) + jnp.dot(r, rest, preferred_element_type=F32)
            )
        return sums

    for m, (lo, hi) in enumerate(SLICES):
        for n in range(1, NSLAB):
            msgs[m, n].wait_recv()
            work[n * MSG + 4 * lo : n * MSG + 4 * hi, :] = recv[n, 4 * lo : 4 * hi, :].astype(F32)
        lax.fori_loop(8 * lo // GROUP, 8 * hi // GROUP, products, 0)
        if hi == 64:
            for e, part in enumerate(route(0, 512)):
                red[pl.ds(e, BLK, stride=4), :] = part
    for e, part in enumerate(route(512, K)):
        red[pl.ds(e, BLK, stride=4), :] = red[pl.ds(e, BLK, stride=4), :] + part
    for b in range(NDEV):
        outs[b] = red[4 * b : 4 * b + 4, :]

    me = i * NSTA + j

    def give(t, _):
        d = lax.rem(me + t, NDEV)
        pltpu.make_async_remote_copy(
            outs.at[d], ins.at[me], rss.at[0], rrs.at[0],
            device_id=(d // NSTA, lax.rem(d, NSTA)), device_id_type=MESH,
        ).start()
        return 0

    def gives(g, _):
        for a in range(7):
            give(1 + g * 7 + a, 0)
        return 0

    lax.fori_loop(0, 18, gives, 0)
    give(127, 0)
    ins[me] = outs[me]
    rest = pl.ds(0, NDEV - 1)
    every = pltpu.make_async_remote_copy(
        outs.at[rest], ins.at[rest], rss.at[0], rrs.at[0], device_id=(i, j), device_id_type=MESH
    )
    every.wait_recv()
    out[...] = jnp.sum(jnp.sum(ins[...].reshape(8, NDEV // 8, 4, BLK), axis=1), axis=0)
    every.wait_send()
    for cp in halos + asks + list(msgs.values()):
        cp.wait_send()


def on_device(model_change, sens_blocks, block_rows, block_cols, live_count, owner_order):
    anyspace = pl.BlockSpec(memory_space=pl.ANY)
    dma = pltpu.SemaphoreType.DMA
    keep = functools.partial(pltpu.with_memory_space_constraint, memory_space=pltpu.HBM)
    vm = pltpu.VMEM
    return pl.pallas_call(
        kernel,
        out_shape=jax.ShapeDtypeStruct((EP, BLK), F32),
        in_specs=[anyspace] * 7,
        out_specs=pl.BlockSpec(memory_space=pltpu.VMEM),
        scratch_shapes=[
            vm((EP, SX, SY, NZ), F32), vm((K, BLK, BLK), BF16), vm((3 * NZ, NZ), BF16),
            vm((1, K), I32), vm((1, K), I32), vm((1, BLK), I32), pltpu.SMEM((1, 1), I32),
            vm((EP, SY, NZ), F32), vm((SX * 4, NZ), F32), vm((8, NZ), F32),
            vm((EP, SY, NZ), F32), vm((SX * 4, NZ), F32), vm((8, NZ), F32),
            vm((2, SX, SY * 4, BLK), F32), vm((CB * 4, BLK), F32),
            vm((CAP // 8, 32, BLK), F32), vm((NSLAB, MSG, BLK), BF16), vm((NSLAB, MSG, BLK), BF16),
            vm((NSLAB * MSG, BLK), F32), vm((GROUP * 4, BLK), F32), vm((K * 4, BLK), F32), vm((BLK, K), BF16),
            vm((NSLAB, 1, BLK), I32), vm((NSLAB, 1, BLK), I32), pltpu.SMEM((NSLAB, 1, BLK), I32),
            vm((2, K), I32), pltpu.SMEM((2, K), I32),
            vm((BLK * 4, BLK), F32), vm((NDEV, 4, BLK), F32), vm((NDEV, 4, BLK), F32),
            dma((9,)), dma((3,)), dma((3,)), dma((NSLAB,)), dma((NSLAB,)),
            dma((len(SLICES) * NSLAB,)), dma((len(SLICES) * NSLAB,)), dma((1,)), dma((1,)),
        ],
        compiler_params=pltpu.CompilerParams(
            collective_id=0, has_side_effects=True, vmem_limit_bytes=52 * 2**20
        ),
        name="gravity_step",
    )(
        keep(model_change),
        keep(sens_blocks.reshape(K, BLK, BLK)),
        keep(block_cols.reshape(1, K)),
        keep(block_rows.reshape(1, K)),
        live_count.reshape(1, 1),
        keep(owner_order.reshape(1, BLK)),
        keep(jnp.asarray(z_matrix())),
    )


def solution(mesh):
    placed = (
        P(None, "slab", "sta", None),
        P("slab", "sta", None, None, None),
        P("slab", "sta", None),
        P("slab", "sta", None),
        P("slab", "sta"),
        P(),
    )
    return jax.shard_map(
        on_device, mesh=mesh, in_specs=placed, out_specs=P(None, ("slab", "sta")), check_vma=False
    )
```

```python
import functools
import math

import jax
import jax.numpy as jnp
import ml_dtypes
import numpy as np
from jax import lax
from jax.experimental import pallas as pl
from jax.experimental.pallas import tpu as pltpu
from jax.sharding import PartitionSpec as P

MESH = pl.DeviceIdType.MESH
F32, BF16, I32 = jnp.float32, jnp.bfloat16, jnp.int32
NT = (((1,), (1,)), ((), ()))
R3 = math.sqrt(3.0)
H0, H1, H2, H3 = (
    (1.0 + R3) / (4.0 * math.sqrt(2.0)),
    (3.0 + R3) / (4.0 * math.sqrt(2.0)),
    (3.0 - R3) / (4.0 * math.sqrt(2.0)),
    (1.0 - R3) / (4.0 * math.sqrt(2.0)),
)
C1, C2 = H3 / H0, H1 / H2

EP, SX, SY, NZ, BLK = 4, 12, 32, 256, 128
K, CAP, CB = 640, 80, 768
NSLAB, NSTA = 16, 8
MSG = CAP * EP
KT = K // BLK
NDEV = NSLAB * NSTA
SLICES = ((0, 24), (24, 48), (48, 64), (64, 80))
GROUP = 64


def torus(step):
    dx, dz = divmod(step, 4)
    return min(dx, 4 - dx) + min(dz, 4 - dz)


STEPS = [(0, 0), (2, 2), (1, 2), (3, 2), (2, 1), (2, 3), (1, 1), (3, 3), (1, 3), (3, 1), (2, 0), (0, 2), (1, 0), (0, 1), (3, 0), (0, 3)]


def z_matrix():
    w = np.zeros((NZ, NZ), np.float64)
    for k in range(NZ // 2):
        src = [(2 * k + d) % NZ for d in range(4)]
        for at, lo, hi in zip(src, (H0, H1, H2, H3), (H3, -H2, H1, -H0)):
            w[at, 2 * k] = lo
            w[at, 2 * k + 1] = hi
    top = w.astype(ml_dtypes.bfloat16)
    rest = (w - top.astype(np.float64)).astype(ml_dtypes.bfloat16)
    return np.concatenate([top, top, rest], 0)


def kernel(
    model, sens, cols, rows, live, owner, wz, out,
    X, sv, wv, cv, rv, ov, lv, Sx, Sy, Sc, Rx, Ry, Rc, D, C, st, send, recv, work, gat, T, R,
    reqv, reqin, reqs, lists, lists_s, red, outs, ins,
    lsem, hss, hrs, qss, qrs, ass_, ars, rss, rrs,
):
    i, j = lax.axis_index("slab"), lax.axis_index("sta")
    xx, zz = i // 4, lax.rem(i, 4)

    loads = [
        pltpu.make_async_copy(src, dst, lsem.at[n])
        for n, (src, dst) in enumerate(
            ((cols, cv), (rows, rv), (owner, ov), (live, lv), (model, X), (wz, wv), (sens, sv))
        )
    ]
    for cp in loads:
        cp.start()

    core = lax.rem(j, 2)

    def partner(n, sign):
        dx, dz = ((sign * d) % 4 for d in STEPS[n])
        mx, mz = (1 * dz) % 4, (1 * dx) % 4
        ax = dx + core * (mx - dx)
        az = dz + core * (mz - dz)
        return lax.rem(xx + ax, 4) * 4 + lax.rem(zz + az, 4)

    ahead = functools.partial(partner, sign=1)
    behind = functools.partial(partner, sign=-1)

    up_i, down_i = lax.rem(i + 1, NSLAB), lax.rem(i + NSLAB - 1, NSLAB)
    up_j, down_j = lax.rem(j + 1, NSTA), lax.rem(j + NSTA - 1, NSTA)

    bar = pltpu.get_barrier_semaphore()
    for n in range(1, NSLAB):
        pl.semaphore_signal(bar, inc=1, device_id=(ahead(n), j), device_id_type=MESH)
    for t in range(1, NSTA):
        pl.semaphore_signal(bar, inc=1, device_id=(i, lax.rem(j + t, NSTA)), device_id_type=MESH)
    pl.semaphore_signal(bar, inc=1, device_id=(up_i, up_j), device_id_type=MESH)

    for cp in loads[:4]:
        cp.wait()
    sub16 = lax.broadcasted_iota(I32, (16, BLK), 0)
    sub128 = lax.broadcasted_iota(I32, (BLK, BLK), 0)
    lane128 = lax.broadcasted_iota(I32, (BLK, BLK), 1)
    sub8 = lax.broadcasted_iota(I32, (8, BLK), 0)
    lane8 = lax.broadcasted_iota(I32, (8, BLK), 1)
    one = lambda m: jnp.where(m, 1.0, 0.0).astype(BF16)
    peer = jnp.zeros((16, BLK), I32)
    for n in range(NSLAB):
        peer = jnp.where(sub16 == n, behind(n), peer)
    first = peer * CB
    upper = one(sub128 < lane128)
    ties, ranks, rels = [], [], []
    carry = jnp.zeros((16, 1), F32)
    for t in range(KT):
        rel = cv[:, t * BLK : (t + 1) * BLK] - first
        tie = (rel >= 0) & (rel < CB)
        tie_f = jnp.where(tie, 1.0, 0.0)
        ranks.append(jnp.dot(tie_f.astype(BF16), upper, preferred_element_type=F32) + carry)
        carry = carry + jnp.sum(tie_f, axis=1, keepdims=True)
        ties.append(tie_f)
        rels.append(jnp.where(tie, rel, 0))
    count = jnp.broadcast_to(carry, (16, BLK))
    bases = []
    for lo, hi in SLICES:
        inside = jnp.clip(count - lo, 0.0, hi - lo)
        scan = inside
        for s in (1, 2, 4, 8):
            scan = scan + jnp.where(sub16 >= s, pltpu.roll(scan, s, 0), 0.0)
        before = jnp.sum(jnp.minimum(count, lo), axis=0, keepdims=True)
        bases.append(before + scan - inside - lo)

    place = one(sub128 == ov[...])
    inverse = lax.dot_general(
        lane8.astype(F32).astype(BF16), place, NT, preferred_element_type=F32
    ).astype(BF16)
    live_now = lv[0, 0]
    ask = jnp.zeros((32, BLK), F32)
    vals, spots = [], []
    for t in range(KT):
        rank_k = jnp.sum(ties[t] * ranks[t], axis=0, keepdims=True).astype(I32)
        slot_k = jnp.sum(ties[t] * (jnp.minimum(ranks[t], CAP - 1.0) + sub16.astype(F32) * CAP), axis=0, keepdims=True).astype(I32)
        base = bases[0]
        for (lo, _), later in zip(SLICES[1:], bases[1:]):
            base = jnp.where(ranks[t] >= lo, later, base)
        spots.append(jnp.sum(ties[t] * (ranks[t] + base), axis=0, keepdims=True).astype(I32))
        rel = rels[t]
        cell = (rel & -64) + ((rel & 1) << 5) + ((rel >> 1) & 31)
        pair = jnp.concatenate([(cell >> 3).astype(F32), (cell & 7).astype(F32)], 0).astype(BF16)
        ask = ask + lax.dot_general(pair, one(sub128 == rank_k), NT, preferred_element_type=F32)
        dest = jnp.dot(
            inverse, one(sub128 == rv[:, t * BLK : (t + 1) * BLK]), preferred_element_type=F32
        )
        here = lane8 + t * BLK
        dest = jnp.where(here < live_now, dest, 128.0)
        slot8 = jnp.broadcast_to(slot_k, (8, BLK))
        val = jnp.where(sub8 == 0, here >> 3, here & 7)
        val = jnp.where(sub8 == 2, slot8 >> 3, val)
        val = jnp.where(sub8 == 3, slot8 & 7, val).astype(F32)
        vals.append(jnp.where(sub8 == 4, dest, val).astype(BF16))
    ask = jnp.clip((ask[:16] * 8.0 + ask[16:]).astype(I32), 0, CB - 1)
    for n in range(NSLAB):
        if n == 0:
            reqin[n] = ask[n : n + 1]
        else:
            reqv[n] = ask[n : n + 1]

    loads[4].wait()
    for e in range(EP):
        Sx[e] = H2 * X[e, 0] + H3 * X[e, 1]
    for e in range(EP):
        for x in range(SX):
            Sy[4 * x + e : 4 * x + e + 1, :] = H2 * X[e, x, 0:1, :] + H3 * X[e, x, 1:2, :]
    Sc[0:4, :] = H2 * Sy[0:4, :] + H3 * Sy[4:8, :]
    Sc[4:8, :] = jnp.zeros((4, NZ), F32)

    pl.semaphore_wait(bar, NSLAB - 1 + NSTA - 1 + 1)
    halos = [
        pltpu.make_async_remote_copy(src, dst, hss.at[n], hrs.at[n], device_id=dev, device_id_type=MESH)
        for n, (src, dst, dev) in enumerate(
            ((Sy, Ry, (i, down_j)), (Sc, Rc, (down_i, down_j)), (Sx, Rx, (down_i, j)))
        )
    ]
    for cp in halos:
        cp.start()
    asks = [
        pltpu.make_async_remote_copy(
            reqv.at[n], reqin.at[n], qss.at[n], qrs.at[n], device_id=(behind(n), j), device_id_type=MESH
        )
        for n in range(1, NSLAB)
    ]
    for cp in asks:
        cp.start()

    def spread(x, e, q, val):
        for z in range(2):
            D[z, x, pl.ds(32 * q + e, 8, stride=4), :] = val[:, z * BLK : (z + 1) * BLK]

    def x_pair(k, _):
        for e in range(EP):
            for q in range(SY // 8):
                at = slice(8 * q, 8 * q + 8)
                s = H0 * X[e, 2 * k, at, :] + H1 * X[e, 2 * k + 1, at, :]
                t = H2 * X[e, 2 * k + 2, at, :] + H3 * X[e, 2 * k + 3, at, :]
                spread(2 * k, e, q, s + t)
                spread(2 * k + 1, e, q, C1 * s + C2 * t)
        return 0

    lax.fori_loop(0, SX // 2 - 1, x_pair, 0)

    order = []
    for u in range(KT):
        got = jnp.zeros((8, BLK), F32)
        for t in range(KT):
            got = got + lax.dot_general(
                vals[t], one(sub128 + u * BLK == spots[t]), NT, preferred_element_type=F32
            )
        dest = got[4:5].astype(I32)
        R[:, u * BLK : (u + 1) * BLK] = one(sub128 == dest)
        lists[0:1, u * BLK : (u + 1) * BLK] = jnp.clip(
            (got[0:1] * 8.0 + got[1:2]).astype(I32), 0, K - 1
        )
        lists[1:2, u * BLK : (u + 1) * BLK] = jnp.clip(
            (got[2:3] * 8.0 + got[3:4]).astype(I32), 0, NSLAB * CAP - 1
        )
    to_s = pltpu.make_async_copy(lists, lists_s, lsem.at[7])
    to_s.start()

    low = lax.broadcasted_iota(I32, (8, BLK), 0) < 4
    ca, cb = jnp.where(low, H0, -H2), jnp.where(low, H1, H3)
    cc, cd = jnp.where(low, H2, -H0), jnp.where(low, H3, H1)
    ce = jnp.where(lax.broadcasted_iota(I32, (8, NZ), 0) < 4, 1.0, C2)
    loads[5].wait()

    def y_inner(x):
        parts = []
        for z in range(2):
            v = D[z, x].reshape(SY // 2, 8, BLK)
            u = pltpu.roll(v, 4, 1)
            t = cc * v[1:] + cd * u[1:]
            none = jnp.zeros((1, 8, BLK), F32)
            parts.append((ca * v + cb * u + jnp.concatenate([t, none], 0)).reshape(SY * 4, BLK))
        return jnp.concatenate(parts, 1)

    def z_pass(full):
        high = full.astype(BF16)
        rest = (full - high.astype(F32)).astype(BF16)
        return jnp.dot(jnp.concatenate([high, rest, high], 1), wv[...], preferred_element_type=F32)

    def yz(x, _):
        res = z_pass(y_inner(x))
        at = pl.multiple_of(x * 2 * SY * 4, 2 * SY * 4)
        C[pl.ds(at, SY * 4), :] = res[:, :BLK]
        C[pl.ds(at + SY * 4, SY * 4), :] = res[:, BLK:]
        return 0

    lax.fori_loop(0, SX - 2, yz, 0)

    for cp in halos:
        cp.wait_recv()
    for e in range(EP):
        for q in range(SY // 8):
            at = slice(8 * q, 8 * q + 8)
            s = H0 * X[e, SX - 2, at, :] + H1 * X[e, SX - 1, at, :]
            t = Rx[e, at, :]
            spread(SX - 2, e, q, s + t)
            spread(SX - 1, e, q, C1 * s + C2 * t)
    lax.fori_loop(SX - 2, SX, yz, 0)
    rims = []
    for k in range(SX // 2):
        s = H0 * Ry[8 * k : 8 * k + 4, :] + H1 * Ry[8 * k + 4 : 8 * k + 8, :]
        if k < SX // 2 - 1:
            t = H2 * Ry[8 * k + 8 : 8 * k + 12, :] + H3 * Ry[8 * k + 12 : 8 * k + 16, :]
        else:
            t = Rc[0:4, :]
        for rim in (s + t, C1 * s + C2 * t):
            rims.append(ce * jnp.concatenate([rim, rim], 0))
    added = z_pass(jnp.concatenate(rims, 0))
    for x in range(SX):
        for z in range(2):
            at = (2 * x + z + 1) * SY * 4 - 8
            C[at : at + 8, :] = C[at : at + 8, :] + added[8 * x : 8 * x + 8, z * BLK : (z + 1) * BLK]

    for cp in asks:
        cp.wait_recv()
    to_r = pltpu.make_async_copy(reqin, reqs, lsem.at[8])
    to_r.start()
    to_r.wait()
    to_s.wait()

    def pack(n, lo, hi):
        def some(g, _):
            for a in range(8):
                c = reqs[n, 0, g * 8 + a]
                st[g, 4 * a : 4 * a + 4, :] = C[pl.ds(c * 4, 4), :]
            return 0

        lax.fori_loop(lo // 8, hi // 8, some, 0)
        return st[lo // 8 : hi // 8].reshape((hi - lo) * 4, BLK).astype(BF16)

    msgs = {}
    for m, (lo, hi) in enumerate(SLICES):
        at = pl.ds(4 * lo, 4 * (hi - lo))
        for n in range(1, NSLAB):
            send[n, at, :] = pack(n, lo, hi)
            sem = m * NSLAB + n
            msgs[m, n] = pltpu.make_async_remote_copy(
                send.at[n, at, :], recv.at[n, at, :], ass_.at[sem], ars.at[sem],
                device_id=(ahead(n), j), device_id_type=MESH,
            )
            msgs[m, n].start()
    work[0:MSG, :] = pack(0, 0, CAP).astype(F32)

    loads[6].wait()
    first_half = lax.broadcasted_iota(I32, (8, BLK), 0) < 4

    def products(g, _):
        for a in range(GROUP):
            c = lists_s[1, g * GROUP + a]
            gat[4 * a : 4 * a + 4, :] = work[pl.ds(c * 4, 4), :]
        for a in range(0, GROUP, 2):
            lhs = gat[4 * a : 4 * a + 8, :].astype(BF16)
            rhs = jnp.concatenate([sv[lists_s[0, g * GROUP + a]], sv[lists_s[0, g * GROUP + a + 1]]], 0)
            res = lax.dot_general(lhs, rhs, NT, preferred_element_type=F32)
            at = pl.multiple_of(g * GROUP * 4, GROUP * 4) + 4 * a
            T[pl.ds(at, 8), :] = jnp.where(first_half, res[:, :BLK], res[:, BLK:])
        return 0

    def route(lo, hi):
        sums = []
        for e in range(EP):
            term = T[pl.ds(lo * 4 + e, hi - lo, stride=4), :]
            high = term.astype(BF16)
            rest = (term - high.astype(F32)).astype(BF16)
            r = R[:, lo:hi]
            sums.append(
                jnp.dot(r, high, preferred_element_type=F32) + jnp.dot(r, rest, preferred_element_type=F32)
            )
        return sums

    for m, (lo, hi) in enumerate(SLICES):
        for n in range(1, NSLAB):
            msgs[m, n].wait_recv()
            work[n * MSG + 4 * lo : n * MSG + 4 * hi, :] = recv[n, 4 * lo : 4 * hi, :].astype(F32)
        lax.fori_loop(8 * lo // GROUP, 8 * hi // GROUP, products, 0)
        if hi == 64:
            for e, part in enumerate(route(0, 512)):
                red[pl.ds(e, BLK, stride=4), :] = part
    for e, part in enumerate(route(512, K)):
        red[pl.ds(e, BLK, stride=4), :] = red[pl.ds(e, BLK, stride=4), :] + part
    for b in range(NDEV):
        outs[b] = red[4 * b : 4 * b + 4, :]

    me = i * NSTA + j

    def give(t, _):
        d = lax.rem(me + t, NDEV)
        pltpu.make_async_remote_copy(
            outs.at[d], ins.at[me], rss.at[0], rrs.at[0],
            device_id=(d // NSTA, lax.rem(d, NSTA)), device_id_type=MESH,
        ).start()
        return 0

    def gives(g, _):
        for a in range(7):
            give(1 + g * 7 + a, 0)
        return 0

    lax.fori_loop(0, 18, gives, 0)
    give(127, 0)
    ins[me] = outs[me]
    rest = pl.ds(0, NDEV - 1)
    every = pltpu.make_async_remote_copy(
        outs.at[rest], ins.at[rest], rss.at[0], rrs.at[0], device_id=(i, j), device_id_type=MESH
    )
    every.wait_recv()
    out[...] = jnp.sum(jnp.sum(ins[...].reshape(8, NDEV // 8, 4, BLK), axis=1), axis=0)
    every.wait_send()
    for cp in halos + asks + list(msgs.values()):
        cp.wait_send()


def on_device(model_change, sens_blocks, block_rows, block_cols, live_count, owner_order):
    anyspace = pl.BlockSpec(memory_space=pl.ANY)
    dma = pltpu.SemaphoreType.DMA
    keep = functools.partial(pltpu.with_memory_space_constraint, memory_space=pltpu.HBM)
    vm = pltpu.VMEM
    return pl.pallas_call(
        kernel,
        out_shape=jax.ShapeDtypeStruct((EP, BLK), F32),
        in_specs=[anyspace] * 7,
        out_specs=pl.BlockSpec(memory_space=pltpu.VMEM),
        scratch_shapes=[
            vm((EP, SX, SY, NZ), F32), vm((K, BLK, BLK), BF16), vm((3 * NZ, NZ), BF16),
            vm((1, K), I32), vm((1, K), I32), vm((1, BLK), I32), pltpu.SMEM((1, 1), I32),
            vm((EP, SY, NZ), F32), vm((SX * 4, NZ), F32), vm((8, NZ), F32),
            vm((EP, SY, NZ), F32), vm((SX * 4, NZ), F32), vm((8, NZ), F32),
            vm((2, SX, SY * 4, BLK), F32), vm((CB * 4, BLK), F32),
            vm((CAP // 8, 32, BLK), F32), vm((NSLAB, MSG, BLK), BF16), vm((NSLAB, MSG, BLK), BF16),
            vm((NSLAB * MSG, BLK), F32), vm((GROUP * 4, BLK), F32), vm((K * 4, BLK), F32), vm((BLK, K), BF16),
            vm((NSLAB, 1, BLK), I32), vm((NSLAB, 1, BLK), I32), pltpu.SMEM((NSLAB, 1, BLK), I32),
            vm((2, K), I32), pltpu.SMEM((2, K), I32),
            vm((BLK * 4, BLK), F32), vm((NDEV, 4, BLK), F32), vm((NDEV, 4, BLK), F32),
            dma((9,)), dma((3,)), dma((3,)), dma((NSLAB,)), dma((NSLAB,)),
            dma((len(SLICES) * NSLAB,)), dma((len(SLICES) * NSLAB,)), dma((1,)), dma((1,)),
        ],
        compiler_params=pltpu.CompilerParams(
            collective_id=0, has_side_effects=True, vmem_limit_bytes=52 * 2**20
        ),
        name="gravity_step",
    )(
        keep(model_change),
        keep(sens_blocks.reshape(K, BLK, BLK)),
        keep(block_cols.reshape(1, K)),
        keep(block_rows.reshape(1, K)),
        live_count.reshape(1, 1),
        keep(owner_order.reshape(1, BLK)),
        keep(jnp.asarray(z_matrix())),
    )


def solution(mesh):
    placed = (
        P(None, "slab", "sta", None),
        P("slab", "sta", None, None, None),
        P("slab", "sta", None),
        P("slab", "sta", None),
        P("slab", "sta"),
        P(),
    )
    return jax.shard_map(
        on_device, mesh=mesh, in_specs=placed, out_specs=P(None, ("slab", "sta")), check_vma=False
    )
```

```python
import functools
import math

import jax
import jax.numpy as jnp
import ml_dtypes
import numpy as np
from jax import lax
from jax.experimental import pallas as pl
from jax.experimental.pallas import tpu as pltpu
from jax.sharding import PartitionSpec as P

MESH = pl.DeviceIdType.MESH
F32, BF16, I32 = jnp.float32, jnp.bfloat16, jnp.int32
NT = (((1,), (1,)), ((), ()))
R3 = math.sqrt(3.0)
H0, H1, H2, H3 = (
    (1.0 + R3) / (4.0 * math.sqrt(2.0)),
    (3.0 + R3) / (4.0 * math.sqrt(2.0)),
    (3.0 - R3) / (4.0 * math.sqrt(2.0)),
    (1.0 - R3) / (4.0 * math.sqrt(2.0)),
)
C1, C2 = H3 / H0, H1 / H2

EP, SX, SY, NZ, BLK = 4, 12, 32, 256, 128
K, CAP, CB = 640, 80, 768
NSLAB, NSTA = 16, 8
MSG = CAP * EP
KT = K // BLK
NDEV = NSLAB * NSTA
SLICES = ((0, 24), (24, 48), (48, 64), (64, 80))
GROUP = 64


def torus(step):
    dx, dz = divmod(step, 4)
    return min(dx, 4 - dx) + min(dz, 4 - dz)


STEPS = [(0, 0), (2, 2), (1, 2), (3, 2), (2, 1), (2, 3), (1, 1), (3, 3), (1, 3), (3, 1), (2, 0), (0, 2), (1, 0), (0, 1), (3, 0), (0, 3)]


def z_matrix():
    w = np.zeros((NZ, NZ), np.float64)
    for k in range(NZ // 2):
        src = [(2 * k + d) % NZ for d in range(4)]
        for at, lo, hi in zip(src, (H0, H1, H2, H3), (H3, -H2, H1, -H0)):
            w[at, 2 * k] = lo
            w[at, 2 * k + 1] = hi
    top = w.astype(ml_dtypes.bfloat16)
    rest = (w - top.astype(np.float64)).astype(ml_dtypes.bfloat16)
    return np.concatenate([top, top, rest], 0)


def kernel(
    model, sens, cols, rows, live, owner, wz, out,
    X, sv, wv, cv, rv, ov, lv, Sx, Sy, Sc, Rx, Ry, Rc, D, C, st, send, recv, work, gat, T, R,
    reqv, reqin, reqs, lists, lists_s, red, outs, ins,
    lsem, hss, hrs, qss, qrs, ass_, ars, rss, rrs,
):
    i, j = lax.axis_index("slab"), lax.axis_index("sta")
    xx, zz = i // 4, lax.rem(i, 4)

    loads = [
        pltpu.make_async_copy(src, dst, lsem.at[n])
        for n, (src, dst) in enumerate(
            ((cols, cv), (rows, rv), (owner, ov), (live, lv), (model, X), (wz, wv), (sens, sv))
        )
    ]
    for cp in loads:
        cp.start()

    core = lax.rem(j, 2)

    def partner(n, sign):
        dx, dz = ((sign * d) % 4 for d in STEPS[n])
        mx, mz = (1 * dz) % 4, (1 * dx) % 4
        ax = dx + core * (mx - dx)
        az = dz + core * (mz - dz)
        return lax.rem(xx + ax, 4) * 4 + lax.rem(zz + az, 4)

    ahead = functools.partial(partner, sign=1)
    behind = functools.partial(partner, sign=-1)

    up_i, down_i = lax.rem(i + 1, NSLAB), lax.rem(i + NSLAB - 1, NSLAB)
    up_j, down_j = lax.rem(j + 1, NSTA), lax.rem(j + NSTA - 1, NSTA)

    bar = pltpu.get_barrier_semaphore()
    for n in range(1, NSLAB):
        pl.semaphore_signal(bar, inc=1, device_id=(ahead(n), j), device_id_type=MESH)
    for t in range(1, NSTA):
        pl.semaphore_signal(bar, inc=1, device_id=(i, lax.rem(j + t, NSTA)), device_id_type=MESH)
    pl.semaphore_signal(bar, inc=1, device_id=(up_i, up_j), device_id_type=MESH)

    for cp in loads[:4]:
        cp.wait()
    sub16 = lax.broadcasted_iota(I32, (16, BLK), 0)
    sub128 = lax.broadcasted_iota(I32, (BLK, BLK), 0)
    lane128 = lax.broadcasted_iota(I32, (BLK, BLK), 1)
    sub8 = lax.broadcasted_iota(I32, (8, BLK), 0)
    lane8 = lax.broadcasted_iota(I32, (8, BLK), 1)
    one = lambda m: jnp.where(m, 1.0, 0.0).astype(BF16)
    peer = jnp.zeros((16, BLK), I32)
    for n in range(NSLAB):
        peer = jnp.where(sub16 == n, behind(n), peer)
    first = peer * CB
    upper = one(sub128 < lane128)
    ties, ranks, rels = [], [], []
    carry = jnp.zeros((16, 1), F32)
    for t in range(KT):
        rel = cv[:, t * BLK : (t + 1) * BLK] - first
        tie = (rel >= 0) & (rel < CB)
        tie_f = jnp.where(tie, 1.0, 0.0)
        ranks.append(jnp.dot(tie_f.astype(BF16), upper, preferred_element_type=F32) + carry)
        carry = carry + jnp.sum(tie_f, axis=1, keepdims=True)
        ties.append(tie_f)
        rels.append(jnp.where(tie, rel, 0))
    count = jnp.broadcast_to(carry, (16, BLK))
    bases = []
    for lo, hi in SLICES:
        inside = jnp.clip(count - lo, 0.0, hi - lo)
        scan = inside
        for s in (1, 2, 4, 8):
            scan = scan + jnp.where(sub16 >= s, pltpu.roll(scan, s, 0), 0.0)
        before = jnp.sum(jnp.minimum(count, lo), axis=0, keepdims=True)
        bases.append(before + scan - inside - lo)

    place = one(sub128 == ov[...])
    inverse = lax.dot_general(
        lane8.astype(F32).astype(BF16), place, NT, preferred_element_type=F32
    ).astype(BF16)
    live_now = lv[0, 0]
    ask = jnp.zeros((32, BLK), F32)
    vals, spots = [], []
    for t in range(KT):
        rank_k = jnp.sum(ties[t] * ranks[t], axis=0, keepdims=True).astype(I32)
        slot_k = jnp.sum(ties[t] * (jnp.minimum(ranks[t], CAP - 1.0) + sub16.astype(F32) * CAP), axis=0, keepdims=True).astype(I32)
        base = bases[0]
        for (lo, _), later in zip(SLICES[1:], bases[1:]):
            base = jnp.where(ranks[t] >= lo, later, base)
        spots.append(jnp.sum(ties[t] * (ranks[t] + base), axis=0, keepdims=True).astype(I32))
        rel = rels[t]
        cell = (rel & -64) + ((rel & 1) << 5) + ((rel >> 1) & 31)
        pair = jnp.concatenate([(cell >> 3).astype(F32), (cell & 7).astype(F32)], 0).astype(BF16)
        ask = ask + lax.dot_general(pair, one(sub128 == rank_k), NT, preferred_element_type=F32)
        dest = jnp.dot(
            inverse, one(sub128 == rv[:, t * BLK : (t + 1) * BLK]), preferred_element_type=F32
        )
        here = lane8 + t * BLK
        dest = jnp.where(here < live_now, dest, 128.0)
        slot8 = jnp.broadcast_to(slot_k, (8, BLK))
        val = jnp.where(sub8 == 0, here >> 3, here & 7)
        val = jnp.where(sub8 == 2, slot8 >> 3, val)
        val = jnp.where(sub8 == 3, slot8 & 7, val).astype(F32)
        vals.append(jnp.where(sub8 == 4, dest, val).astype(BF16))
    ask = jnp.clip((ask[:16] * 8.0 + ask[16:]).astype(I32), 0, CB - 1)
    for n in range(NSLAB):
        if n == 0:
            reqin[n] = ask[n : n + 1]
        else:
            reqv[n] = ask[n : n + 1]

    loads[4].wait()
    for e in range(EP):
        Sx[e] = H2 * X[e, 0] + H3 * X[e, 1]
    for e in range(EP):
        for x in range(SX):
            Sy[4 * x + e : 4 * x + e + 1, :] = H2 * X[e, x, 0:1, :] + H3 * X[e, x, 1:2, :]
    Sc[0:4, :] = H2 * Sy[0:4, :] + H3 * Sy[4:8, :]
    Sc[4:8, :] = jnp.zeros((4, NZ), F32)

    pl.semaphore_wait(bar, NSLAB - 1 + NSTA - 1 + 1)
    halos = [
        pltpu.make_async_remote_copy(src, dst, hss.at[n], hrs.at[n], device_id=dev, device_id_type=MESH)
        for n, (src, dst, dev) in enumerate(
            ((Sy, Ry, (i, down_j)), (Sc, Rc, (down_i, down_j)), (Sx, Rx, (down_i, j)))
        )
    ]
    for cp in halos:
        cp.start()
    asks = [
        pltpu.make_async_remote_copy(
            reqv.at[n], reqin.at[n], qss.at[n], qrs.at[n], device_id=(behind(n), j), device_id_type=MESH
        )
        for n in range(1, NSLAB)
    ]
    for cp in asks:
        cp.start()

    def spread(x, e, q, val):
        for z in range(2):
            D[z, x, pl.ds(32 * q + e, 8, stride=4), :] = val[:, z * BLK : (z + 1) * BLK]

    def x_pair(k, _):
        for e in range(EP):
            for q in range(SY // 8):
                at = slice(8 * q, 8 * q + 8)
                s = H0 * X[e, 2 * k, at, :] + H1 * X[e, 2 * k + 1, at, :]
                t = H2 * X[e, 2 * k + 2, at, :] + H3 * X[e, 2 * k + 3, at, :]
                spread(2 * k, e, q, s + t)
                spread(2 * k + 1, e, q, C1 * s + C2 * t)
        return 0

    lax.fori_loop(0, SX // 2 - 1, x_pair, 0)

    order = []
    for u in range(KT):
        got = jnp.zeros((8, BLK), F32)
        for t in range(KT):
            got = got + lax.dot_general(
                vals[t], one(sub128 + u * BLK == spots[t]), NT, preferred_element_type=F32
            )
        dest = got[4:5].astype(I32)
        R[:, u * BLK : (u + 1) * BLK] = one(sub128 == dest)
        lists[0:1, u * BLK : (u + 1) * BLK] = jnp.clip(
            (got[0:1] * 8.0 + got[1:2]).astype(I32), 0, K - 1
        )
        lists[1:2, u * BLK : (u + 1) * BLK] = jnp.clip(
            (got[2:3] * 8.0 + got[3:4]).astype(I32), 0, NSLAB * CAP - 1
        )
    to_s = pltpu.make_async_copy(lists, lists_s, lsem.at[7])
    to_s.start()

    low = lax.broadcasted_iota(I32, (8, BLK), 0) < 4
    ca, cb = jnp.where(low, H0, -H2), jnp.where(low, H1, H3)
    cc, cd = jnp.where(low, H2, -H0), jnp.where(low, H3, H1)
    ce = jnp.where(lax.broadcasted_iota(I32, (8, NZ), 0) < 4, 1.0, C2)
    loads[5].wait()

    def y_inner(x):
        parts = []
        for z in range(2):
            v = D[z, x].reshape(SY // 2, 8, BLK)
            u = pltpu.roll(v, 4, 1)
            t = cc * v[1:] + cd * u[1:]
            none = jnp.zeros((1, 8, BLK), F32)
            parts.append((ca * v + cb * u + jnp.concatenate([t, none], 0)).reshape(SY * 4, BLK))
        return jnp.concatenate(parts, 1)

    def z_pass(full):
        high = full.astype(BF16)
        rest = (full - high.astype(F32)).astype(BF16)
        return jnp.dot(jnp.concatenate([high, rest, high], 1), wv[...], preferred_element_type=F32)

    def yz(x, _):
        res = z_pass(y_inner(x))
        at = pl.multiple_of(x * 2 * SY * 4, 2 * SY * 4)
        C[pl.ds(at, SY * 4), :] = res[:, :BLK]
        C[pl.ds(at + SY * 4, SY * 4), :] = res[:, BLK:]
        return 0

    lax.fori_loop(0, SX - 2, yz, 0)

    for cp in halos:
        cp.wait_recv()
    for e in range(EP):
        for q in range(SY // 8):
            at = slice(8 * q, 8 * q + 8)
            s = H0 * X[e, SX - 2, at, :] + H1 * X[e, SX - 1, at, :]
            t = Rx[e, at, :]
            spread(SX - 2, e, q, s + t)
            spread(SX - 1, e, q, C1 * s + C2 * t)
    lax.fori_loop(SX - 2, SX, yz, 0)
    rims = []
    for k in range(SX // 2):
        s = H0 * Ry[8 * k : 8 * k + 4, :] + H1 * Ry[8 * k + 4 : 8 * k + 8, :]
        if k < SX // 2 - 1:
            t = H2 * Ry[8 * k + 8 : 8 * k + 12, :] + H3 * Ry[8 * k + 12 : 8 * k + 16, :]
        else:
            t = Rc[0:4, :]
        for rim in (s + t, C1 * s + C2 * t):
            rims.append(ce * jnp.concatenate([rim, rim], 0))
    added = z_pass(jnp.concatenate(rims, 0))
    for x in range(SX):
        for z in range(2):
            at = (2 * x + z + 1) * SY * 4 - 8
            C[at : at + 8, :] = C[at : at + 8, :] + added[8 * x : 8 * x + 8, z * BLK : (z + 1) * BLK]

    for cp in asks:
        cp.wait_recv()
    to_r = pltpu.make_async_copy(reqin, reqs, lsem.at[8])
    to_r.start()
    to_r.wait()
    to_s.wait()

    def pack(n, lo, hi):
        def some(g, _):
            for a in range(8):
                c = reqs[n, 0, g * 8 + a]
                st[g, 4 * a : 4 * a + 4, :] = C[pl.ds(c * 4, 4), :]
            return 0

        lax.fori_loop(lo // 8, hi // 8, some, 0)
        return st[lo // 8 : hi // 8].reshape((hi - lo) * 4, BLK).astype(BF16)

    msgs = {}
    for m, (lo, hi) in enumerate(SLICES):
        at = pl.ds(4 * lo, 4 * (hi - lo))
        for n in range(1, NSLAB):
            send[n, at, :] = pack(n, lo, hi)
            sem = m * NSLAB + n
            msgs[m, n] = pltpu.make_async_remote_copy(
                send.at[n, at, :], recv.at[n, at, :], ass_.at[sem], ars.at[sem],
                device_id=(ahead(n), j), device_id_type=MESH,
            )
            msgs[m, n].start()
    work[0:MSG, :] = pack(0, 0, CAP).astype(F32)

    loads[6].wait()
    first_half = lax.broadcasted_iota(I32, (8, BLK), 0) < 4

    def products(g, _):
        for a in range(GROUP):
            c = lists_s[1, g * GROUP + a]
            gat[4 * a : 4 * a + 4, :] = work[pl.ds(c * 4, 4), :]
        for a in range(0, GROUP, 2):
            lhs = gat[4 * a : 4 * a + 8, :].astype(BF16)
            rhs = jnp.concatenate([sv[lists_s[0, g * GROUP + a]], sv[lists_s[0, g * GROUP + a + 1]]], 0)
            res = lax.dot_general(lhs, rhs, NT, preferred_element_type=F32)
            at = pl.multiple_of(g * GROUP * 4, GROUP * 4) + 4 * a
            T[pl.ds(at, 8), :] = jnp.where(first_half, res[:, :BLK], res[:, BLK:])
        return 0

    def route(lo, hi):
        sums = []
        for e in range(EP):
            term = T[pl.ds(lo * 4 + e, hi - lo, stride=4), :]
            high = term.astype(BF16)
            rest = (term - high.astype(F32)).astype(BF16)
            r = R[:, lo:hi]
            sums.append(
                jnp.dot(r, high, preferred_element_type=F32) + jnp.dot(r, rest, preferred_element_type=F32)
            )
        return sums

    for m, (lo, hi) in enumerate(SLICES):
        for n in range(1, NSLAB):
            msgs[m, n].wait_recv()
            work[n * MSG + 4 * lo : n * MSG + 4 * hi, :] = recv[n, 4 * lo : 4 * hi, :].astype(F32)
        lax.fori_loop(8 * lo // GROUP, 8 * hi // GROUP, products, 0)
        if hi == 64:
            for e, part in enumerate(route(0, 512)):
                red[pl.ds(e, BLK, stride=4), :] = part
    for e, part in enumerate(route(512, K)):
        red[pl.ds(e, BLK, stride=4), :] = red[pl.ds(e, BLK, stride=4), :] + part
    for b in range(NDEV):
        outs[b] = red[4 * b : 4 * b + 4, :]

    me = i * NSTA + j

    def give(t, _):
        d = lax.rem(me + t, NDEV)
        pltpu.make_async_remote_copy(
            outs.at[d], ins.at[me], rss.at[0], rrs.at[0],
            device_id=(d // NSTA, lax.rem(d, NSTA)), device_id_type=MESH,
        ).start()
        return 0

    def gives(g, _):
        for a in range(7):
            give(1 + g * 7 + a, 0)
        return 0

    lax.fori_loop(0, 18, gives, 0)
    give(127, 0)
    ins[me] = outs[me]
    rest = pl.ds(0, NDEV - 1)
    every = pltpu.make_async_remote_copy(
        outs.at[rest], ins.at[rest], rss.at[0], rrs.at[0], device_id=(i, j), device_id_type=MESH
    )
    for cp in halos + asks + list(msgs.values()):
        cp.wait_send()
    every.wait_recv()
    out[...] = jnp.sum(jnp.sum(ins[...].reshape(8, NDEV // 8, 4, BLK), axis=1), axis=0)
    every.wait_send()


def on_device(model_change, sens_blocks, block_rows, block_cols, live_count, owner_order):
    anyspace = pl.BlockSpec(memory_space=pl.ANY)
    dma = pltpu.SemaphoreType.DMA
    keep = functools.partial(pltpu.with_memory_space_constraint, memory_space=pltpu.HBM)
    vm = pltpu.VMEM
    return pl.pallas_call(
        kernel,
        out_shape=jax.ShapeDtypeStruct((EP, BLK), F32),
        in_specs=[anyspace] * 7,
        out_specs=pl.BlockSpec(memory_space=pltpu.VMEM),
        scratch_shapes=[
            vm((EP, SX, SY, NZ), F32), vm((K, BLK, BLK), BF16), vm((3 * NZ, NZ), BF16),
            vm((1, K), I32), vm((1, K), I32), vm((1, BLK), I32), pltpu.SMEM((1, 1), I32),
            vm((EP, SY, NZ), F32), vm((SX * 4, NZ), F32), vm((8, NZ), F32),
            vm((EP, SY, NZ), F32), vm((SX * 4, NZ), F32), vm((8, NZ), F32),
            vm((2, SX, SY * 4, BLK), F32), vm((CB * 4, BLK), F32),
            vm((CAP // 8, 32, BLK), F32), vm((NSLAB, MSG, BLK), BF16), vm((NSLAB, MSG, BLK), BF16),
            vm((NSLAB * MSG, BLK), F32), vm((GROUP * 4, BLK), F32), vm((K * 4, BLK), F32), vm((BLK, K), BF16),
            vm((NSLAB, 1, BLK), I32), vm((NSLAB, 1, BLK), I32), pltpu.SMEM((NSLAB, 1, BLK), I32),
            vm((2, K), I32), pltpu.SMEM((2, K), I32),
            vm((BLK * 4, BLK), F32), vm((NDEV, 4, BLK), F32), vm((NDEV, 4, BLK), F32),
            dma((9,)), dma((3,)), dma((3,)), dma((NSLAB,)), dma((NSLAB,)),
            dma((len(SLICES) * NSLAB,)), dma((len(SLICES) * NSLAB,)), dma((1,)), dma((1,)),
        ],
        compiler_params=pltpu.CompilerParams(
            collective_id=0, has_side_effects=True, vmem_limit_bytes=52 * 2**20
        ),
        name="gravity_step",
    )(
        keep(model_change),
        keep(sens_blocks.reshape(K, BLK, BLK)),
        keep(block_cols.reshape(1, K)),
        keep(block_rows.reshape(1, K)),
        live_count.reshape(1, 1),
        keep(owner_order.reshape(1, BLK)),
        keep(jnp.asarray(z_matrix())),
    )


def solution(mesh):
    placed = (
        P(None, "slab", "sta", None),
        P("slab", "sta", None, None, None),
        P("slab", "sta", None),
        P("slab", "sta", None),
        P("slab", "sta"),
        P(),
    )
    return jax.shard_map(
        on_device, mesh=mesh, in_specs=placed, out_specs=P(None, ("slab", "sta")), check_vma=False
    )
```
